32 devices in a mesh: groups: 2 (over y), rows: 4 (over z), cols: 4 (over x, core).
Axes of the slice: x: 2, y: 2, z: 4, core: 2. Of those that a mesh axis runs over, the one named last changes fastest.
Arguments:
- hidden: bfloat16 [64, 32, 1280], P(('groups', 'rows'), 'cols'), parts along dimension 0, may hold values from -6 to 6
- ln_gain: float32 [1280], replicated, may hold values from 0.1 to 1.9
- ln_bias: float32 [1280], replicated, may hold values from -3 to 3
- w_query: bfloat16 [1280, 256], P(None, 'cols'), may hold values from -8.944272 to 8.944272
- w_keyval: bfloat16 [1280, 512], P(None, 'cols'), may hold values from -0.3125 to 0.3125
- stale_keyval: bfloat16 [64, 32, 4, 128], P(('groups', 'rows'), None, 'cols'), parts along dimension 0, may hold values from -10 to 10
- w_out: bfloat16 [256, 1280], replicated, may hold values from -0.375 to 0.375
- out_bias: float32 [1280], replicated, may hold values from -3 to 3
Outputs:
- output_rows: bfloat16 [64, 32, 1280], P(('groups', 'rows'), 'cols'), parts along dimension 0
- fresh_keyval: bfloat16 [64, 32, 4, 128], P(('groups', 'rows'), None, 'cols'), parts along dimension 0
The draws below stay inside these ranges and needn't reach their ends.
There are 2 independent parts, one for each index of `groups`. The reference program is written for one: setup_inputs(seed, part) draws one part's arguments, and reference() takes and returns one part's arrays. A program takes and returns all parts, laid end to end along the dimension named above; an argument that names none is the same for every part. Nothing has to cross between parts.
All inputs are finite; a program needn't handle non-finite values.
Results may differ from the reference program's by a relative error of at most 0.04.
The reference program's roundings to bfloat16 on the way count: a program that leaves them out, or rounds other values in their place, can miss the bound.
Values may be sent and summed in bfloat16 or wider, within the bound.
A program may use at most 64 MiB of HBM per device.

```python
import math
import jax
import jax.numpy as jnp
from jax import lax

D = 1280
HD = 64
RB = 8
HEADS = 4
H = 32
W = 32
N_ROWS = 4


def draw_w_query(key, part):
    values = jnp.clip(jax.random.normal(key, (D, HEADS * HD), jnp.float32), -4.0, 4.0) * (2.0 / math.sqrt(D))
    return values.astype(jnp.bfloat16)


def block_levels(stream_key, shape, shards, smallest, top_value):
    def one(dim, shards_of):
        heights = jax.random.uniform(jax.random.fold_in(jax.random.fold_in(stream_key, 6), dim), (shards_of,), jnp.float32, smallest / len(shards), top_value / len(shards))
        return jnp.repeat(jnp.exp(heights), shape[dim] // shards_of).reshape((-1,) + (1,) * (len(shape) - dim - 1))

    factor_of = one(*shards[0])
    for cut in shards[1:]:
        factor_of = factor_of * one(*cut)
    return factor_of


def bell_draw(own_key, shape, deviation, reach, split=(), kind=jnp.bfloat16):
    array = deviation * jax.random.normal(own_key, shape, jnp.float32)
    if split:
        array = array * block_levels(own_key, shape, split, -0.22, 0.18)
    return jnp.clip(array, -reach, reach).astype(kind)


def setup_inputs(seed: int = 0, part: int = 0) -> dict:
    seeds = jax.random.split(jax.random.key(seed), 9)
    own_keys = jax.random.split(jax.random.fold_in(seeds[8], part), 9)
    hidden = bell_draw(own_keys[0], (H, W, D), 1.0, 6.0, ((0, 4), (1, 4)))
    ln_gain = jnp.clip(1.0 + 0.18 * jax.random.normal(seeds[1], (D,), jnp.float32), 0.1, 1.9)
    ln_bias = bell_draw(seeds[2], (D,), 0.5, 3.0, (), jnp.float32)
    w_query = draw_w_query(jax.random.fold_in(seeds[8], 71), part)
    w_keyval = bell_draw(seeds[4], (D, HEADS * 2 * HD), (D // 4) ** -0.5, 0.3125, ((1, 4),))
    stale_keyval = bell_draw(own_keys[5], (H, W, HEADS, 2 * HD), 2.0, 10.0, ((0, 4), (2, 4)))
    w_out = bell_draw(seeds[6], (HEADS * HD, D), (HEADS * HD) ** -0.5, 0.375)
    out_bias = bell_draw(seeds[7], (D,), 0.5, 3.0, (), jnp.float32)
    return dict(hidden=hidden, ln_gain=ln_gain, ln_bias=ln_bias, w_query=w_query, w_keyval=w_keyval, stale_keyval=stale_keyval, w_out=w_out, out_bias=out_bias)


def layer_norm(hidden, ln_gain, ln_bias):
    values = hidden.astype(jnp.float32)
    row_mean = lax.optimization_barrier(jnp.mean(values, axis=-1, keepdims=True))
    centred = values - row_mean
    variance = lax.optimization_barrier(jnp.mean(centred * centred, axis=-1, keepdims=True))
    return (centred * lax.rsqrt(variance + 1e-05) * ln_gain + ln_bias).astype(jnp.bfloat16)

def reference(hidden, ln_gain, ln_bias, w_query, w_keyval, stale_keyval, w_out, out_bias):
    rows_all, cols_all, channels = hidden.shape
    normed = layer_norm(hidden, ln_gain, ln_bias).reshape(-1, channels)
    queries = jnp.dot(normed, w_query, preferred_element_type=jnp.float32).astype(jnp.bfloat16)
    queries = queries.reshape(rows_all, cols_all, HEADS, HD)
    keyval = jnp.dot(normed, w_keyval, preferred_element_type=jnp.float32).astype(jnp.bfloat16)
    keyval = keyval.reshape(rows_all, cols_all, HEADS, 2 * HD)
    score_scale = 1.0 / math.sqrt(HD)

    def one_task(position):
        band_index = (position // HEADS).astype(jnp.int32)
        head_index = (position % HEADS).astype(jnp.int32)
        first_row = (band_index * RB).astype(jnp.int32)
        head_queries = lax.dynamic_index_in_dim(queries, head_index, 2, keepdims=False)
        band_queries = lax.dynamic_slice_in_dim(head_queries, first_row, RB, 0).reshape(RB * cols_all, HD)
        stale_keys = lax.dynamic_index_in_dim(stale_keyval, head_index, 2, keepdims=False)
        fresh_keys = lax.dynamic_slice_in_dim(lax.dynamic_index_in_dim(keyval, head_index, 2, keepdims=False), first_row, RB, 0)
        merged = lax.dynamic_update_slice_in_dim(stale_keys, fresh_keys, first_row, 0).reshape(-1, 2 * HD)
        scores = jnp.dot(band_queries, merged[:, :HD].T, preferred_element_type=jnp.float32) * score_scale
        row_max = lax.optimization_barrier(jnp.max(scores, axis=-1, keepdims=True))
        weights = jnp.exp(scores - row_max)
        denominator = lax.optimization_barrier(jnp.sum(weights, axis=-1, keepdims=True))
        summed = jnp.dot(weights.astype(jnp.bfloat16), merged[:, HD:], preferred_element_type=jnp.float32)
        return (summed / denominator).astype(jnp.bfloat16)
    attention = lax.map(one_task, jnp.arange(N_ROWS * HEADS, dtype=jnp.int32))
    attention = attention.reshape(N_ROWS, HEADS, RB, cols_all, HD).transpose(0, 2, 3, 1, 4)
    attention = attention.reshape(rows_all * cols_all, HEADS * HD)
    projected = jnp.dot(attention, w_out, preferred_element_type=jnp.float32)
    output_rows = projected + out_bias + hidden.reshape(-1, channels).astype(jnp.float32)
    output_rows = output_rows.astype(jnp.bfloat16).reshape(rows_all, cols_all, channels)
    return (output_rows, keyval)
```

```python
import functools
import math

import jax
import jax.numpy as jnp
from jax import lax
from jax.experimental import pallas as pl
from jax.experimental.pallas import tpu as pltpu
from jax.sharding import PartitionSpec as P

MESH = pl.DeviceIdType.MESH
PIECES = 4


def repeat(count, body):
    if count <= 4:
        for index in range(count):
            body(index)
    else:
        lax.fori_loop(0, count, lambda index, carry: (body(index), carry)[1], 0)


def kernel(
    n_rows, n_cols, cores,
    hidden_hbm, gain_ref, bias_ref, w_query_hbm, w_keyval_hbm, stale_hbm, w_out_hbm, out_bias_ref,
    out_hbm, fresh_hbm,
    hidden, w_query, w_keyval, w_out, normed, queries, keyval, fresh_wide, fresh, out, attention,
    load_sem, band_send, band_recv, strip_send, strip_recv, relay_send, relay_recv, att_send, att_recv, store_sem,
):
    row = lax.axis_index("rows")
    col = lax.axis_index("cols")
    chips = n_cols // cores
    chip, core = col // cores, col % cores
    sibling = chip * cores + (cores - 1 - core)
    band_rows, strip_cols, channels = hidden.shape
    strip = band_rows * strip_cols
    pair = cores * strip
    head_size = w_query.shape[1]
    piece = strip // PIECES
    scale = 1.0 / math.sqrt(head_size)

    loads = [
        pltpu.make_async_copy(source, target, load_sem.at[index])
        for index, (source, target) in enumerate(
            [
                (hidden_hbm, hidden),
                (w_query_hbm, w_query),
                (w_keyval_hbm, w_keyval),
                (w_out_hbm, w_out),
            ]
        )
    ]
    for load in loads:
        load.start()

    barrier = pltpu.get_barrier_semaphore()

    def greet_col(step):
        pl.semaphore_signal(
            barrier, inc=1, device_id={"cols": lax.rem(col + step + 1, n_cols)}, device_id_type=MESH
        )

    def greet_row(step):
        pl.semaphore_signal(
            barrier, inc=1, device_id={"rows": lax.rem(row + step + 1, n_rows)}, device_id_type=MESH
        )

    repeat(n_cols - 1, greet_col)
    repeat(n_rows - 1, greet_row)

    loads[0].wait()
    values = hidden[...].astype(jnp.float32).reshape(strip, channels)
    centred = values - jnp.mean(values, axis=-1, keepdims=True)
    variance = jnp.mean(centred * centred, axis=-1, keepdims=True)
    own_rows = pl.ds(pl.multiple_of(core * strip, strip), strip)
    normed[chip, own_rows, :] = (
        centred * lax.rsqrt(variance + 1e-05) * gain_ref[...] + bias_ref[...]
    ).astype(jnp.bfloat16)
    pl.semaphore_wait(barrier, n_cols - 1 + n_rows - 1)

    def rows_of(core_index, part):
        return pl.ds(pl.multiple_of(core_index * strip + part * piece, piece), piece)

    def strip_copy(step, part):
        other = lax.rem(chip + step + 1, chips)
        block = normed.at[chip, rows_of(core, part), :]
        return pltpu.make_async_remote_copy(
            src_ref=block, dst_ref=block,
            send_sem=strip_send.at[step, part], recv_sem=strip_recv.at[step, part],
            device_id={"cols": other * cores + core}, device_id_type=MESH,
        )

    def relay_copy(step, part):
        source_chip = lax.rem(chip + chips - step, chips)
        block = normed.at[source_chip, rows_of(core, part), :]
        return pltpu.make_async_remote_copy(
            src_ref=block, dst_ref=block,
            send_sem=relay_send.at[step, part], recv_sem=relay_recv.at[step, part],
            device_id={"cols": sibling}, device_id_type=MESH,
        )

    def band_copy(step):
        return pltpu.make_async_remote_copy(
            src_ref=stale_hbm, dst_ref=keyval.at[row],
            send_sem=band_send.at[step], recv_sem=band_recv.at[step],
            device_id={"rows": lax.rem(row + step + 1, n_rows)}, device_id_type=MESH,
        )

    for part in range(PIECES):
        repeat(chips - 1, lambda step, part=part: strip_copy(step, part).start())
    if cores > 1:
        for part in range(PIECES):
            relay_copy(0, part).start()
    repeat(n_rows - 1, lambda step: band_copy(step).start())

    def project(index):
        rows = normed[index]
        own = jnp.dot(rows, w_query[...], preferred_element_type=jnp.float32).astype(jnp.bfloat16)
        queries[index] = jnp.concatenate([own, jnp.zeros_like(own)], axis=1)
        both = jnp.dot(rows, w_keyval[...], preferred_element_type=jnp.float32).astype(jnp.bfloat16)
        keyval[row, pl.ds(pl.multiple_of(index * pair, pair), pair), :] = both
        wide = both.astype(jnp.float32).reshape(cores, band_rows, strip_cols, both.shape[1])
        for which in range(cores):
            fresh_wide[:, index * cores + which] = wide[which]

    for load in loads[1:3]:
        load.wait()
    if cores > 1:
        for part in range(PIECES):
            relay_copy(0, part).wait_recv()
    project(chip)

    def arrive(step):
        for part in range(PIECES):
            strip_copy(step, part).wait_recv()
            if cores > 1:
                relay_copy(step + 1, part).start()
        if cores > 1:
            for part in range(PIECES):
                relay_copy(step + 1, part).wait_recv()
        project(lax.rem(chip + chips - step - 1, chips))

    repeat(chips - 1, arrive)

    fresh[...] = fresh_wide[...].reshape(fresh.shape).astype(jnp.bfloat16)
    fresh_store = pltpu.make_async_copy(fresh, fresh_hbm, store_sem.at[0])
    fresh_store.start()

    repeat(n_rows - 1, lambda step: band_copy(step).wait_recv())

    cells = keyval.shape[1]
    together = max(size for size in range(1, n_rows + 1) if n_rows % size == 0 and (size == 1 or size * cells <= 1024))

    def absorb(own, index):
        block = keyval[pl.ds(index * together, together)].reshape(together * cells, keyval.shape[2])
        scores = lax.dot_general(
            own, block, (((1,), (1,)), ((), ())), preferred_element_type=jnp.float32
        )
        return block, scores

    def attend(index):
        own = queries[index]
        if together == n_rows:
            block, scores = absorb(own, 0)
            row_max = jnp.max(scores, axis=-1, keepdims=True)
            weights = jnp.exp((scores - row_max) * scale)
            denominator = jnp.sum(weights, axis=-1, keepdims=True)
            weighted = jnp.dot(weights.astype(jnp.bfloat16), block, preferred_element_type=jnp.float32)
        else:

            def body(step, state):
                row_max, denominator, weighted = state
                block, scores = absorb(own, step)
                new_max = jnp.maximum(row_max, jnp.max(scores, axis=-1, keepdims=True))
                factor = jnp.exp((row_max - new_max) * scale)
                weights = jnp.exp((scores - new_max) * scale)
                return (
                    new_max,
                    denominator * factor + jnp.sum(weights, axis=-1, keepdims=True),
                    weighted * factor
                    + jnp.dot(weights.astype(jnp.bfloat16), block, preferred_element_type=jnp.float32),
                )

            initial = (
                jnp.full((pair, 1), -1e30, jnp.float32),
                jnp.zeros((pair, 1), jnp.float32),
                jnp.zeros((pair, 2 * head_size), jnp.float32),
            )
            row_max, denominator, weighted = lax.fori_loop(0, n_rows // together, body, initial)
        return (weighted[:, head_size:] / denominator).astype(jnp.bfloat16)

    def att_copy(target, step):
        return pltpu.make_async_remote_copy(
            src_ref=attention.at[0, target], dst_ref=attention.at[1, col],
            send_sem=att_send.at[step], recv_sem=att_recv.at[step],
            device_id={"cols": target}, device_id_type=MESH,
        )

    def serve(step):
        other = lax.rem(chip + step + 1, chips)
        found = attend(other)
        for which in range(cores):
            target = other * cores + lax.rem(core + which, cores)
            attention[0, other * cores + which] = found[which * strip : (which + 1) * strip]
        for which in range(cores):
            target = other * cores + lax.rem(core + which, cores)
            att_copy(target, (step + 1) * cores + which).start()

    repeat(chips - 1, serve)
    found = attend(chip)
    for which in range(cores):
        attention[0, chip * cores + which] = found[which * strip : (which + 1) * strip]
    if cores > 1:
        att_copy(sibling, 1).start()
    attention[1, col] = attention[0, col]

    loads[3].wait()
    if cores > 1:
        att_copy(sibling, 1).wait_recv()
    for step in range(cores, n_cols):
        att_copy(sibling, step).wait_recv()
    together_heads = jnp.concatenate([attention[1, head] for head in range(n_cols)], axis=1)
    result = jnp.dot(together_heads, w_out[...], preferred_element_type=jnp.float32)
    result = result + out_bias_ref[...] + hidden[...].astype(jnp.float32).reshape(strip, channels)
    out[...] = result.reshape(out.shape).astype(jnp.bfloat16)
    out_store = pltpu.make_async_copy(out, out_hbm, store_sem.at[1])
    out_store.start()

    for part in range(PIECES):
        repeat(chips - 1, lambda step, part=part: strip_copy(step, part).wait_send())
        if cores > 1:
            repeat(chips, lambda step, part=part: relay_copy(step, part).wait_send())
    repeat(n_rows - 1, lambda step: band_copy(step).wait_send())
    for step in range(1, n_cols):
        att_copy(sibling, step).wait_send()
    fresh_store.wait()
    out_store.wait()


def shards(n_rows, n_cols, hidden, ln_gain, ln_bias, w_query, w_keyval, stale_keyval, w_out, out_bias):
    band_rows, strip_cols, channels = hidden.shape
    head_size = w_query.shape[1]
    full_cols = stale_keyval.shape[1]
    cells = band_rows * full_cols
    strip = band_rows * strip_cols
    cores = 2 if n_cols % 2 == 0 else 1
    chips = n_cols // cores
    bf16, f32 = jnp.bfloat16, jnp.float32
    anywhere = pl.BlockSpec(memory_space=pl.ANY)
    near = pl.BlockSpec(memory_space=pltpu.VMEM)
    dma = pltpu.SemaphoreType.DMA
    out, fresh = pl.pallas_call(
        functools.partial(kernel, n_rows, n_cols, cores),
        out_shape=(
            jax.ShapeDtypeStruct(hidden.shape, bf16),
            jax.ShapeDtypeStruct((band_rows, full_cols, 2 * head_size), bf16),
        ),
        in_specs=[anywhere, near, near, anywhere, anywhere, anywhere, anywhere, near],
        out_specs=(anywhere, anywhere),
        scratch_shapes=[
            pltpu.VMEM(hidden.shape, bf16),
            pltpu.VMEM(w_query.shape, bf16),
            pltpu.VMEM(w_keyval.shape, bf16),
            pltpu.VMEM(w_out.shape, bf16),
            pltpu.VMEM((chips, cores * strip, channels), bf16),
            pltpu.VMEM((chips, cores * strip, 2 * head_size), bf16),
            pltpu.VMEM((n_rows, cells, 2 * head_size), bf16),
            pltpu.VMEM((band_rows, n_cols, strip_cols, 2 * head_size), f32),
            pltpu.VMEM((band_rows, full_cols, 2 * head_size), bf16),
            pltpu.VMEM(hidden.shape, bf16),
            pltpu.VMEM((2, n_cols, strip, head_size), bf16),
            dma((4,)),
            dma((n_rows,)),
            dma((n_rows,)),
            dma((chips, PIECES)),
            dma((chips, PIECES)),
            dma((chips, PIECES)),
            dma((chips, PIECES)),
            dma((n_cols,)),
            dma((n_cols,)),
            dma((2,)),
        ],
        compiler_params=pltpu.CompilerParams(
            collective_id=0, has_side_effects=True, vmem_limit_bytes=48 * 1024 * 1024
        ),
    )(
        hidden,
        ln_gain.reshape(1, channels),
        ln_bias.reshape(1, channels),
        w_query,
        w_keyval,
        stale_keyval.reshape(cells, 2 * head_size),
        w_out,
        out_bias.reshape(1, channels),
    )
    return out, fresh.reshape(band_rows, full_cols, 1, 2 * head_size)


def solution(mesh):
    return jax.shard_map(
        functools.partial(shards, mesh.shape["rows"], mesh.shape["cols"]),
        mesh=mesh,
        in_specs=(
            P(("groups", "rows"), "cols", None),
            P(),
            P(),
            P(None, "cols"),
            P(None, "cols"),
            P(("groups", "rows"), None, "cols", None),
            P(),
            P(),
        ),
        out_specs=(P(("groups", "rows"), "cols", None), P(("groups", "rows"), None, "cols", None)),
        check_vma=False,
    )
```

```python
import functools
import math

import jax
import jax.numpy as jnp
from jax import lax
from jax.experimental import pallas as pl
from jax.experimental.pallas import tpu as pltpu
from jax.sharding import PartitionSpec as P

MESH = pl.DeviceIdType.MESH
PIECES = 4


def repeat(count, body):
    if count <= 4:
        for index in range(count):
            body(index)
    else:
        lax.fori_loop(0, count, lambda index, carry: (body(index), carry)[1], 0)


def kernel(
    n_rows, n_cols, cores,
    hidden_hbm, gain_hbm, bias_hbm, w_query_hbm, w_keyval_hbm, stale_hbm, w_out_hbm, out_bias_hbm,
    out_hbm, fresh_hbm,
    hidden, gain, bias, out_bias, w_query, w_keyval, w_out, normed, queries, keyval, fresh_wide, fresh, out, attention,
    load_sem, band_send, band_recv, strip_send, strip_recv, relay_send, relay_recv, att_send, att_recv, store_sem,
):
    row = lax.axis_index("rows")
    col = lax.axis_index("cols")
    chips = n_cols // cores
    chip, core = col // cores, col % cores
    sibling = chip * cores + (cores - 1 - core)
    band_rows, strip_cols, channels = hidden.shape
    strip = band_rows * strip_cols
    pair = cores * strip
    head_size = w_query.shape[0]
    piece = strip // PIECES
    scale = 1.0 / math.sqrt(head_size)

    loads = [
        pltpu.make_async_copy(source, target, load_sem.at[index])
        for index, (source, target) in enumerate(
            [
                (hidden_hbm, hidden),
                (gain_hbm, gain),
                (bias_hbm, bias),
                (w_query_hbm, w_query),
                (w_keyval_hbm, w_keyval),
                (w_out_hbm, w_out),
                (out_bias_hbm, out_bias),
            ]
        )
    ]
    for load in loads:
        load.start()

    barrier = pltpu.get_barrier_semaphore()

    def greet_col(step):
        pl.semaphore_signal(
            barrier, inc=1, device_id={"cols": lax.rem(col + step + 1, n_cols)}, device_id_type=MESH
        )

    def greet_row(step):
        pl.semaphore_signal(
            barrier, inc=1, device_id={"rows": lax.rem(row + step + 1, n_rows)}, device_id_type=MESH
        )

    repeat(n_cols - 1, greet_col)
    repeat(n_rows - 1, greet_row)

    def rows_of(core_index, part):
        return pl.ds(pl.multiple_of(core_index * strip + part * piece, piece), piece)

    def strip_copy(step, part):
        other = lax.rem(chip + step + 1, chips)
        block = normed.at[chip, rows_of(core, part), :]
        return pltpu.make_async_remote_copy(
            src_ref=block, dst_ref=block,
            send_sem=strip_send.at[step, part], recv_sem=strip_recv.at[step, part],
            device_id={"cols": other * cores + core}, device_id_type=MESH,
        )

    def relay_copy(step, part):
        source_chip = lax.rem(chip + chips - step, chips)
        block = normed.at[source_chip, rows_of(core, part), :]
        return pltpu.make_async_remote_copy(
            src_ref=block, dst_ref=block,
            send_sem=relay_send.at[step, part], recv_sem=relay_recv.at[step, part],
            device_id={"cols": sibling}, device_id_type=MESH,
        )

    def band_copy(step):
        return pltpu.make_async_remote_copy(
            src_ref=stale_hbm, dst_ref=keyval.at[row],
            send_sem=band_send.at[step], recv_sem=band_recv.at[step],
            device_id={"rows": lax.rem(row + step + 1, n_rows)}, device_id_type=MESH,
        )

    pl.semaphore_wait(barrier, n_cols - 1 + n_rows - 1)
    repeat(n_rows - 1, lambda step: band_copy(step).start())

    for load in loads[:3]:
        load.wait()
    gains, biases = gain[...].reshape(1, channels), bias[...].reshape(1, channels)
    piece_rows = band_rows // PIECES
    for part in range(PIECES):
        values = hidden[part * piece_rows : (part + 1) * piece_rows].astype(jnp.float32)
        values = values.reshape(piece, channels)
        centred = values - jnp.mean(values, axis=-1, keepdims=True)
        variance = jnp.mean(centred * centred, axis=-1, keepdims=True)
        normed[chip, rows_of(core, part), :] = (
            centred * lax.rsqrt(variance + 1e-05) * gains + biases
        ).astype(jnp.bfloat16)
        repeat(chips - 1, lambda step: strip_copy(step, part).start())
        if cores > 1:
            relay_copy(0, part).start()

    def project(index):
        rows = normed[index]
        own = lax.dot_general(
            rows, w_query[...], (((1,), (1,)), ((), ())), preferred_element_type=jnp.float32
        ).astype(jnp.bfloat16)
        queries[index] = jnp.concatenate([own, jnp.zeros_like(own)], axis=1)
        both = jnp.dot(rows, w_keyval[...], preferred_element_type=jnp.float32).astype(jnp.bfloat16)
        keyval[row, pl.ds(pl.multiple_of(index * pair, pair), pair), :] = both
        wide = both.astype(jnp.float32).reshape(cores, band_rows, strip_cols, both.shape[1])
        for which in range(cores):
            fresh_wide[:, index * cores + which] = wide[which]

    for load in loads[3:5]:
        load.wait()
    if cores > 1:
        for part in range(PIECES):
            relay_copy(0, part).wait_recv()
    project(chip)

    def arrive(step):
        for part in range(PIECES):
            strip_copy(step, part).wait_recv()
            if cores > 1:
                relay_copy(step + 1, part).start()
        if cores > 1:
            for part in range(PIECES):
                relay_copy(step + 1, part).wait_recv()
        project(lax.rem(chip + chips - step - 1, chips))

    repeat(chips - 1, arrive)

    fresh[...] = fresh_wide[...].reshape(fresh.shape).astype(jnp.bfloat16)
    fresh_store = pltpu.make_async_copy(fresh, fresh_hbm, store_sem.at[0])
    fresh_store.start()

    repeat(n_rows - 1, lambda step: band_copy(step).wait_recv())

    cells = keyval.shape[1]
    together = max(size for size in range(1, n_rows + 1) if n_rows % size == 0 and (size == 1 or size * cells <= 1024))

    def absorb(own, index):
        block = keyval[pl.ds(index * together, together)].reshape(together * cells, keyval.shape[2])
        scores = lax.dot_general(
            own, block, (((1,), (1,)), ((), ())), preferred_element_type=jnp.float32
        )
        return block, scores

    def attend(index):
        own = queries[index]
        if together == n_rows:
            block, scores = absorb(own, 0)
            row_max = jnp.max(scores, axis=-1, keepdims=True)
            weights = jnp.exp((scores - row_max) * scale)
            denominator = jnp.sum(weights, axis=-1, keepdims=True)
            weighted = jnp.dot(weights.astype(jnp.bfloat16), block, preferred_element_type=jnp.float32)
        else:

            def body(step, state):
                row_max, denominator, weighted = state
                block, scores = absorb(own, step)
                new_max = jnp.maximum(row_max, jnp.max(scores, axis=-1, keepdims=True))
                factor = jnp.exp((row_max - new_max) * scale)
                weights = jnp.exp((scores - new_max) * scale)
                return (
                    new_max,
                    denominator * factor + jnp.sum(weights, axis=-1, keepdims=True),
                    weighted * factor
                    + jnp.dot(weights.astype(jnp.bfloat16), block, preferred_element_type=jnp.float32),
                )

            initial = (
                jnp.full((pair, 1), -1e30, jnp.float32),
                jnp.zeros((pair, 1), jnp.float32),
                jnp.zeros((pair, 2 * head_size), jnp.float32),
            )
            row_max, denominator, weighted = lax.fori_loop(0, n_rows // together, body, initial)
        return (weighted[:, head_size:] / denominator).astype(jnp.bfloat16)

    def att_copy(target, step):
        return pltpu.make_async_remote_copy(
            src_ref=attention.at[0, target], dst_ref=attention.at[1, col],
            send_sem=att_send.at[step], recv_sem=att_recv.at[step],
            device_id={"cols": target}, device_id_type=MESH,
        )

    def serve(step):
        other = lax.rem(chip + step + 1, chips)
        found = attend(other)
        for which in range(cores):
            target = other * cores + lax.rem(core + which, cores)
            attention[0, other * cores + which] = found[which * strip : (which + 1) * strip]
        for which in range(cores):
            target = other * cores + lax.rem(core + which, cores)
            att_copy(target, (step + 1) * cores + which).start()

    repeat(chips - 1, serve)
    found = attend(chip)
    for which in range(cores):
        attention[0, chip * cores + which] = found[which * strip : (which + 1) * strip]
    if cores > 1:
        att_copy(sibling, 1).start()
    attention[1, col] = attention[0, col]

    for load in loads[5:]:
        load.wait()
    if cores > 1:
        att_copy(sibling, 1).wait_recv()
    for step in range(cores, n_cols):
        att_copy(sibling, step).wait_recv()
    together_heads = jnp.concatenate([attention[1, head] for head in range(n_cols)], axis=1)
    result = jnp.dot(together_heads, w_out[...], preferred_element_type=jnp.float32)
    result = result + out_bias[...].reshape(1, channels) + hidden[...].astype(jnp.float32).reshape(strip, channels)
    out[...] = result.reshape(out.shape).astype(jnp.bfloat16)
    out_store = pltpu.make_async_copy(out, out_hbm, store_sem.at[1])
    out_store.start()

    for part in range(PIECES):
        repeat(chips - 1, lambda step, part=part: strip_copy(step, part).wait_send())
        if cores > 1:
            repeat(chips, lambda step, part=part: relay_copy(step, part).wait_send())
    repeat(n_rows - 1, lambda step: band_copy(step).wait_send())
    for step in range(1, n_cols):
        att_copy(sibling, step).wait_send()
    fresh_store.wait()
    out_store.wait()


def shards(n_rows, n_cols, hidden, ln_gain, ln_bias, w_query, w_keyval, stale_keyval, w_out, out_bias):
    band_rows, strip_cols, channels = hidden.shape
    head_size = w_query.shape[1]
    full_cols = stale_keyval.shape[1]
    cells = band_rows * full_cols
    strip = band_rows * strip_cols
    cores = 2 if n_cols % 2 == 0 else 1
    chips = n_cols // cores
    bf16, f32 = jnp.bfloat16, jnp.float32
    far = pl.BlockSpec(memory_space=pltpu.HBM)
    dma = pltpu.SemaphoreType.DMA
    out, fresh = pl.pallas_call(
        functools.partial(kernel, n_rows, n_cols, cores),
        out_shape=(
            jax.ShapeDtypeStruct(hidden.shape, bf16),
            jax.ShapeDtypeStruct((band_rows, full_cols, 2 * head_size), bf16),
        ),
        in_specs=[far] * 8,
        out_specs=(far, far),
        scratch_shapes=[
            pltpu.VMEM(hidden.shape, bf16),
            pltpu.VMEM((channels,), f32),
            pltpu.VMEM((channels,), f32),
            pltpu.VMEM((channels,), f32),
            pltpu.VMEM((head_size, channels), bf16),
            pltpu.VMEM(w_keyval.shape, bf16),
            pltpu.VMEM(w_out.shape, bf16),
            pltpu.VMEM((chips, cores * strip, channels), bf16),
            pltpu.VMEM((chips, cores * strip, 2 * head_size), bf16),
            pltpu.VMEM((n_rows, cells, 2 * head_size), bf16),
            pltpu.VMEM((band_rows, n_cols, strip_cols, 2 * head_size), f32),
            pltpu.VMEM((band_rows, full_cols, 2 * head_size), bf16),
            pltpu.VMEM(hidden.shape, bf16),
            pltpu.VMEM((2, n_cols, strip, head_size), bf16),
            dma((7,)),
            dma((n_rows,)),
            dma((n_rows,)),
            dma((chips, PIECES)),
            dma((chips, PIECES)),
            dma((chips, PIECES)),
            dma((chips, PIECES)),
            dma((n_cols,)),
            dma((n_cols,)),
            dma((2,)),
        ],
        compiler_params=pltpu.CompilerParams(
            collective_id=0, has_side_effects=True, vmem_limit_bytes=64 * 1024 * 1024
        ),
    )(
        hidden,
        ln_gain,
        ln_bias,
        w_query.T,
        w_keyval,
        stale_keyval.reshape(cells, 2 * head_size),
        w_out,
        out_bias,
    )
    return out, fresh.reshape(band_rows, full_cols, 1, 2 * head_size)


def solution(mesh):
    return jax.shard_map(
        functools.partial(shards, mesh.shape["rows"], mesh.shape["cols"]),
        mesh=mesh,
        in_specs=(
            P(("groups", "rows"), "cols", None),
            P(),
            P(),
            P(None, "cols"),
            P(None, "cols"),
            P(("groups", "rows"), None, "cols", None),
            P(),
            P(),
        ),
        out_specs=(P(("groups", "rows"), "cols", None), P(("groups", "rows"), None, "cols", None)),
        check_vma=False,
    )
```

```python
import functools
import math

import jax
import jax.numpy as jnp
from jax import lax
from jax.experimental import pallas as pl
from jax.experimental.pallas import tpu as pltpu
from jax.sharding import PartitionSpec as P

MESH = pl.DeviceIdType.MESH
PIECES = 4


def repeat(count, body):
    if count <= 4:
        for index in range(count):
            body(index)
    else:
        lax.fori_loop(0, count, lambda index, carry: (body(index), carry)[1], 0)


def kernel(
    n_rows, n_cols, cores,
    hidden_hbm, gain_hbm, bias_hbm, w_query_hbm, w_keyval_hbm, stale_hbm, w_out_hbm, out_bias_hbm,
    out, fresh,
    hidden, gain, bias, out_bias, w_query, w_keyval, w_out, normed, queries, keyval, fresh_wide, attention,
    load_sem, band_send, band_recv, strip_send, strip_recv, relay_send, relay_recv, att_send, att_recv,
):
    row = lax.axis_index("rows")
    col = lax.axis_index("cols")
    chips = n_cols // cores
    chip, core = col // cores, col % cores
    sibling = chip * cores + (cores - 1 - core)
    band_rows, strip_cols, channels = hidden.shape
    strip = band_rows * strip_cols
    pair = cores * strip
    head_size = w_query.shape[0]
    piece = strip // PIECES
    scale = 1.0 / math.sqrt(head_size)

    loads = [
        pltpu.make_async_copy(source, target, load_sem.at[index])
        for index, (source, target) in enumerate(
            [
                (hidden_hbm, hidden),
                (gain_hbm, gain),
                (bias_hbm, bias),
                (w_query_hbm, w_query),
                (w_keyval_hbm, w_keyval),
                (w_out_hbm, w_out),
                (out_bias_hbm, out_bias),
            ]
        )
    ]
    for load in loads:
        load.start()

    barrier = pltpu.get_barrier_semaphore()

    def greet_col(step):
        pl.semaphore_signal(
            barrier, inc=1, device_id={"cols": lax.rem(col + step + 1, n_cols)}, device_id_type=MESH
        )

    def greet_row(step):
        pl.semaphore_signal(
            barrier, inc=1, device_id={"rows": lax.rem(row + step + 1, n_rows)}, device_id_type=MESH
        )

    repeat(n_cols - 1, greet_col)
    repeat(n_rows - 1, greet_row)

    def rows_of(core_index, part):
        return pl.ds(pl.multiple_of(core_index * strip + part * piece, piece), piece)

    def strip_copy(step, part):
        other = lax.rem(chip + step + 1, chips)
        block = normed.at[chip, rows_of(core, part), :]
        return pltpu.make_async_remote_copy(
            src_ref=block, dst_ref=block,
            send_sem=strip_send.at[step, part], recv_sem=strip_recv.at[step, part],
            device_id={"cols": other * cores + core}, device_id_type=MESH,
        )

    def relay_copy(step, part):
        source_chip = lax.rem(chip + chips - step, chips)
        block = normed.at[source_chip, rows_of(core, part), :]
        return pltpu.make_async_remote_copy(
            src_ref=block, dst_ref=block,
            send_sem=relay_send.at[step, part], recv_sem=relay_recv.at[step, part],
            device_id={"cols": sibling}, device_id_type=MESH,
        )

    def band_copy(step):
        return pltpu.make_async_remote_copy(
            src_ref=stale_hbm, dst_ref=keyval.at[row],
            send_sem=band_send.at[step], recv_sem=band_recv.at[step],
            device_id={"rows": lax.rem(row + step + 1, n_rows)}, device_id_type=MESH,
        )

    pl.semaphore_wait(barrier, n_cols - 1 + n_rows - 1)
    repeat(n_rows - 1, lambda step: band_copy(step).start())

    for load in loads[:3]:
        load.wait()
    gains, biases = gain[...].reshape(1, channels), bias[...].reshape(1, channels)
    piece_rows = band_rows // PIECES
    for part in range(PIECES):
        values = hidden[part * piece_rows : (part + 1) * piece_rows].astype(jnp.float32)
        values = values.reshape(piece, channels)
        centred = values - jnp.mean(values, axis=-1, keepdims=True)
        variance = jnp.mean(centred * centred, axis=-1, keepdims=True)
        normed[chip, rows_of(core, part), :] = (
            centred * lax.rsqrt(variance + 1e-05) * gains + biases
        ).astype(jnp.bfloat16)
        repeat(chips - 1, lambda step: strip_copy(step, part).start())
        if cores > 1:
            relay_copy(0, part).start()

    def project(index):
        rows = normed[index]
        own = lax.dot_general(
            rows, w_query[...], (((1,), (1,)), ((), ())), preferred_element_type=jnp.float32
        ).astype(jnp.bfloat16)
        queries[index] = jnp.concatenate([own, jnp.zeros_like(own)], axis=1)
        both = jnp.dot(rows, w_keyval[...], preferred_element_type=jnp.float32).astype(jnp.bfloat16)
        keyval[row, pl.ds(pl.multiple_of(index * pair, pair), pair), :] = both
        wide = both.astype(jnp.float32).reshape(cores, band_rows, strip_cols, both.shape[1])
        for which in range(cores):
            fresh_wide[:, index * cores + which] = wide[which]

    for load in loads[3:5]:
        load.wait()
    if cores > 1:
        for part in range(PIECES):
            relay_copy(0, part).wait_recv()
    project(chip)

    def arrive(step):
        for part in range(PIECES):
            strip_copy(step, part).wait_recv()
            if cores > 1:
                relay_copy(step + 1, part).start()
        if cores > 1:
            for part in range(PIECES):
                relay_copy(step + 1, part).wait_recv()
        project(lax.rem(chip + chips - step - 1, chips))

    repeat(chips - 1, arrive)

    fresh[...] = fresh_wide[...].reshape(fresh.shape).astype(jnp.bfloat16)

    repeat(n_rows - 1, lambda step: band_copy(step).wait_recv())

    cells = keyval.shape[1]
    together = max(size for size in range(1, n_rows + 1) if n_rows % size == 0 and (size == 1 or size * cells <= 1024))

    def absorb(own, index):
        block = keyval[pl.ds(index * together, together)].reshape(together * cells, keyval.shape[2])
        scores = lax.dot_general(
            own, block, (((1,), (1,)), ((), ())), preferred_element_type=jnp.float32
        )
        return block, scores

    def attend(index):
        own = queries[index]
        if together == n_rows:
            block, scores = absorb(own, 0)
            row_max = jnp.max(scores, axis=-1, keepdims=True)
            weights = jnp.exp((scores - row_max) * scale)
            denominator = jnp.sum(weights, axis=-1, keepdims=True)
            weighted = jnp.dot(weights.astype(jnp.bfloat16), block, preferred_element_type=jnp.float32)
        else:

            def body(step, state):
                row_max, denominator, weighted = state
                block, scores = absorb(own, step)
                new_max = jnp.maximum(row_max, jnp.max(scores, axis=-1, keepdims=True))
                factor = jnp.exp((row_max - new_max) * scale)
                weights = jnp.exp((scores - new_max) * scale)
                return (
                    new_max,
                    denominator * factor + jnp.sum(weights, axis=-1, keepdims=True),
                    weighted * factor
                    + jnp.dot(weights.astype(jnp.bfloat16), block, preferred_element_type=jnp.float32),
                )

            initial = (
                jnp.full((pair, 1), -1e30, jnp.float32),
                jnp.zeros((pair, 1), jnp.float32),
                jnp.zeros((pair, 2 * head_size), jnp.float32),
            )
            row_max, denominator, weighted = lax.fori_loop(0, n_rows // together, body, initial)
        return (weighted[:, head_size:] / denominator).astype(jnp.bfloat16)

    def att_copy(target, step):
        return pltpu.make_async_remote_copy(
            src_ref=attention.at[0, target], dst_ref=attention.at[1, col],
            send_sem=att_send.at[step], recv_sem=att_recv.at[step],
            device_id={"cols": target}, device_id_type=MESH,
        )

    def serve(step):
        other = lax.rem(chip + step + 1, chips)
        found = attend(other)
        for which in range(cores):
            target = other * cores + lax.rem(core + which, cores)
            attention[0, other * cores + which] = found[which * strip : (which + 1) * strip]
        for which in range(cores):
            target = other * cores + lax.rem(core + which, cores)
            att_copy(target, (step + 1) * cores + which).start()

    repeat(chips - 1, serve)
    found = attend(chip)
    for which in range(cores):
        attention[0, chip * cores + which] = found[which * strip : (which + 1) * strip]
    if cores > 1:
        att_copy(sibling, 1).start()
    attention[1, col] = attention[0, col]

    for load in loads[5:]:
        load.wait()
    if cores > 1:
        att_copy(sibling, 1).wait_recv()
    for step in range(cores, n_cols):
        att_copy(sibling, step).wait_recv()
    together_heads = jnp.concatenate([attention[1, head] for head in range(n_cols)], axis=1)
    result = jnp.dot(together_heads, w_out[...], preferred_element_type=jnp.float32)
    result = result + out_bias[...].reshape(1, channels) + hidden[...].astype(jnp.float32).reshape(strip, channels)
    out[...] = result.reshape(out.shape).astype(jnp.bfloat16)

    for part in range(PIECES):
        repeat(chips - 1, lambda step, part=part: strip_copy(step, part).wait_send())
        if cores > 1:
            repeat(chips, lambda step, part=part: relay_copy(step, part).wait_send())
    repeat(n_rows - 1, lambda step: band_copy(step).wait_send())
    for step in range(1, n_cols):
        att_copy(sibling, step).wait_send()


def write_back(out, fresh, out_hbm, fresh_hbm, store_sem):
    stores = [
        pltpu.make_async_copy(out, out_hbm, store_sem.at[0]),
        pltpu.make_async_copy(fresh, fresh_hbm, store_sem.at[1]),
    ]
    for store in stores:
        store.start()
    for store in stores:
        store.wait()


def shards(n_rows, n_cols, hidden, ln_gain, ln_bias, w_query, w_keyval, stale_keyval, w_out, out_bias):
    band_rows, strip_cols, channels = hidden.shape
    head_size = w_query.shape[1]
    full_cols = stale_keyval.shape[1]
    cells = band_rows * full_cols
    strip = band_rows * strip_cols
    cores = 2 if n_cols % 2 == 0 else 1
    chips = n_cols // cores
    bf16, f32 = jnp.bfloat16, jnp.float32
    near = pl.BlockSpec(memory_space=pltpu.VMEM)
    far = pl.BlockSpec(memory_space=pltpu.HBM)
    dma = pltpu.SemaphoreType.DMA
    operands = (
        hidden,
        ln_gain,
        ln_bias,
        w_query.T,
        w_keyval,
        stale_keyval.reshape(cells, 2 * head_size),
        w_out,
        out_bias,
    )
    shapes = (hidden.shape, (band_rows, full_cols, 2 * head_size))
    found = pl.pallas_call(
        functools.partial(kernel, n_rows, n_cols, cores),
        out_shape=tuple(pltpu.VMEM(shape, bf16) for shape in shapes),
        in_specs=[far] * 8,
        out_specs=(near, near),
        scratch_shapes=[
            pltpu.VMEM(hidden.shape, bf16),
            pltpu.VMEM((channels,), f32),
            pltpu.VMEM((channels,), f32),
            pltpu.VMEM((channels,), f32),
            pltpu.VMEM((head_size, channels), bf16),
            pltpu.VMEM(w_keyval.shape, bf16),
            pltpu.VMEM(w_out.shape, bf16),
            pltpu.VMEM((chips, cores * strip, channels), bf16),
            pltpu.VMEM((chips, cores * strip, 2 * head_size), bf16),
            pltpu.VMEM((n_rows, cells, 2 * head_size), bf16),
            pltpu.VMEM((band_rows, n_cols, strip_cols, 2 * head_size), f32),
            pltpu.VMEM((2, n_cols, strip, head_size), bf16),
            dma((7,)),
            dma((n_rows,)),
            dma((n_rows,)),
            dma((chips, PIECES)),
            dma((chips, PIECES)),
            dma((chips, PIECES)),
            dma((chips, PIECES)),
            dma((n_cols,)),
            dma((n_cols,)),
        ],
        compiler_params=pltpu.CompilerParams(
            collective_id=0, has_side_effects=True, vmem_limit_bytes=48 * 1024 * 1024
        ),
    )(*(pltpu.with_memory_space_constraint(operand, pltpu.HBM) for operand in operands))
    out, fresh = pl.pallas_call(
        write_back,
        out_shape=tuple(pltpu.HBM(shape, bf16) for shape in shapes),
        in_specs=[near, near],
        out_specs=(far, far),
        scratch_shapes=[dma((2,))],
    )(*found)
    return out, fresh.reshape(band_rows, full_cols, 1, 2 * head_size)


def solution(mesh):
    return jax.shard_map(
        functools.partial(shards, mesh.shape["rows"], mesh.shape["cols"]),
        mesh=mesh,
        in_specs=(
            P(("groups", "rows"), "cols", None),
            P(),
            P(),
            P(None, "cols"),
            P(None, "cols"),
            P(("groups", "rows"), None, "cols", None),
            P(),
            P(),
        ),
        out_specs=(P(("groups", "rows"), "cols", None), P(("groups", "rows"), None, "cols", None)),
        check_vma=False,
    )
```

```python
import functools
import math

import jax
import jax.numpy as jnp
from jax import lax
from jax.experimental import pallas as pl
from jax.experimental.pallas import tpu as pltpu
from jax.sharding import PartitionSpec as P

MESH = pl.DeviceIdType.MESH
PIECES = 4
HALVES = 2


def repeat(count, body):
    if count <= 4:
        for index in range(count):
            body(index)
    else:
        lax.fori_loop(0, count, lambda index, carry: (body(index), carry)[1], 0)


def kernel(
    n_rows, n_cols, cores,
    hidden_hbm, gain_hbm, bias_hbm, w_query_hbm, w_keyval_hbm, stale_hbm, w_out_hbm, out_bias_hbm,
    out, fresh,
    hidden, gain, bias, out_bias, w_query, w_keyval, w_out, normed, queries, keyval, fresh_wide, attention,
    load_sem, right_send, right_recv, left_send, left_recv, strip_send, strip_recv, relay_send, relay_recv, att_send, att_recv,
):
    row = lax.axis_index("rows")
    col = lax.axis_index("cols")
    chips = n_cols // cores
    chip, core = col // cores, col % cores
    sibling = chip * cores + (cores - 1 - core)
    band_rows, strip_cols, channels = hidden.shape
    strip = band_rows * strip_cols
    pair = cores * strip
    head_size = w_query.shape[0]
    piece = strip // PIECES
    scale = 1.0 / math.sqrt(head_size)

    loads = [
        pltpu.make_async_copy(source, target, load_sem.at[index])
        for index, (source, target) in enumerate(
            [
                (hidden_hbm, hidden),
                (gain_hbm, gain),
                (bias_hbm, bias),
                (w_query_hbm, w_query),
                (w_keyval_hbm, w_keyval),
                (w_out_hbm, w_out),
                (out_bias_hbm, out_bias),
            ]
        )
    ]
    for load in loads:
        load.start()

    barrier = pltpu.get_barrier_semaphore()

    def greet_col(step):
        pl.semaphore_signal(
            barrier, inc=1, device_id={"cols": lax.rem(col + step + 1, n_cols)}, device_id_type=MESH
        )

    def greet_row(other):
        pl.semaphore_signal(barrier, inc=1, device_id={"rows": other}, device_id_type=MESH)

    has_left, has_right = row >= 1, row + 1 < n_rows
    pl.when(has_left)(lambda: greet_row(row - 1))
    pl.when(has_right)(lambda: greet_row(row + 1))
    repeat(n_cols - 1, greet_col)

    def rows_of(core_index, part):
        return pl.ds(pl.multiple_of(core_index * strip + part * piece, piece), piece)

    def strip_copy(step, part):
        other = lax.rem(chip + step + 1, chips)
        block = normed.at[chip, rows_of(core, part), :]
        return pltpu.make_async_remote_copy(
            src_ref=block, dst_ref=block,
            send_sem=strip_send.at[step, part], recv_sem=strip_recv.at[step, part],
            device_id={"cols": other * cores + core}, device_id_type=MESH,
        )

    def relay_copy(step, part):
        source_chip = lax.rem(chip + chips - step, chips)
        block = normed.at[source_chip, rows_of(core, part), :]
        return pltpu.make_async_remote_copy(
            src_ref=block, dst_ref=block,
            send_sem=relay_send.at[step, part], recv_sem=relay_recv.at[step, part],
            device_id={"cols": sibling}, device_id_type=MESH,
        )

    half_cells = keyval.shape[1] // HALVES

    def right_copy(distance, half):
        place = pl.ds(half * half_cells, half_cells)
        source = stale_hbm.at[place] if isinstance(distance, int) and distance == 0 else keyval.at[row - distance, place]
        return pltpu.make_async_remote_copy(
            src_ref=source, dst_ref=keyval.at[row - distance, place],
            send_sem=right_send.at[distance, half], recv_sem=right_recv.at[distance, half],
            device_id={"rows": lax.rem(row + 1, n_rows)}, device_id_type=MESH,
        )

    def left_copy(distance, half):
        place = pl.ds(half * half_cells, half_cells)
        source = stale_hbm.at[place] if isinstance(distance, int) and distance == 0 else keyval.at[row + distance, place]
        return pltpu.make_async_remote_copy(
            src_ref=source, dst_ref=keyval.at[row + distance, place],
            send_sem=left_send.at[distance, half], recv_sem=left_recv.at[distance, half],
            device_id={"rows": lax.rem(row + n_rows - 1, n_rows)}, device_id_type=MESH,
        )

    def arrived(recv_sem, source, distance, half):
        block = keyval.at[source, pl.ds(half * half_cells, half_cells)]
        pltpu.make_async_copy(block, block, recv_sem.at[distance - 1, half]).wait()

    def hand_on(distance, half):
        @pl.when(row >= distance)
        def from_left():
            arrived(right_recv, row - distance, distance, half)
            pl.when(has_right)(lambda: right_copy(distance, half).start())

        @pl.when(row + distance < n_rows)
        def from_right():
            arrived(left_recv, row + distance, distance, half)
            pl.when(has_left)(lambda: left_copy(distance, half).start())

    def handed_on(distance, half):
        pl.when((row >= distance) & has_right)(lambda: right_copy(distance, half).wait_send())
        pl.when((row + distance < n_rows) & has_left)(lambda: left_copy(distance, half).wait_send())

    neighbours = has_left.astype(jnp.int32) + has_right.astype(jnp.int32)
    pl.semaphore_wait(barrier, n_cols - 1 + neighbours)
    for half in range(HALVES):
        pl.when(has_right)(lambda half=half: right_copy(0, half).start())
        pl.when(has_left)(lambda half=half: left_copy(0, half).start())

    for load in loads[:3]:
        load.wait()
    gains, biases = gain[...].reshape(1, channels), bias[...].reshape(1, channels)
    piece_rows = band_rows // PIECES
    for part in range(PIECES):
        values = hidden[part * piece_rows : (part + 1) * piece_rows].astype(jnp.float32)
        values = values.reshape(piece, channels)
        centred = values - jnp.mean(values, axis=-1, keepdims=True)
        variance = jnp.mean(centred * centred, axis=-1, keepdims=True)
        normed[chip, rows_of(core, part), :] = (
            centred * lax.rsqrt(variance + 1e-05) * gains + biases
        ).astype(jnp.bfloat16)
        repeat(chips - 1, lambda step: strip_copy(step, part).start())
        if cores > 1:
            relay_copy(0, part).start()

    def project(index):
        rows = normed[index]
        own = lax.dot_general(
            rows, w_query[...], (((1,), (1,)), ((), ())), preferred_element_type=jnp.float32
        ).astype(jnp.bfloat16)
        queries[index] = jnp.concatenate([own, jnp.zeros_like(own)], axis=1)
        both = jnp.dot(rows, w_keyval[...], preferred_element_type=jnp.float32).astype(jnp.bfloat16)
        keyval[row, pl.ds(pl.multiple_of(index * pair, pair), pair), :] = both
        wide = both.astype(jnp.float32).reshape(cores, band_rows, strip_cols, both.shape[1])
        for which in range(cores):
            fresh_wide[:, index * cores + which] = wide[which]

    for load in loads[3:5]:
        load.wait()
    if cores > 1:
        for part in range(PIECES):
            relay_copy(0, part).wait_recv()
    project(chip)

    few = n_rows <= 4
    if few:
        pending = [(distance, half) for distance in range(1, n_rows) for half in range(HALVES)]
    else:
        pending = []

    def arrive(step):
        for part in range(PIECES):
            if pending and pending[0][0] < n_rows - 1:
                hand_on(*pending.pop(0))
            strip_copy(step, part).wait_recv()
            if cores > 1:
                relay_copy(step + 1, part).start()
        if cores > 1:
            for part in range(PIECES):
                relay_copy(step + 1, part).wait_recv()
        project(lax.rem(chip + chips - step - 1, chips))

    if not few:

        @pl.loop(1, n_rows)
        def hand_all_on(distance):
            for half in range(HALVES):
                hand_on(distance, half)

    repeat(chips - 1, arrive)
    for distance, half in pending:
        hand_on(distance, half)

    fresh[...] = fresh_wide[...].reshape(fresh.shape).astype(jnp.bfloat16)

    cells = keyval.shape[1]
    together = max(size for size in range(1, n_rows + 1) if n_rows % size == 0 and (size == 1 or size * cells <= 1024))

    def absorb(own, index):
        block = keyval[pl.ds(index * together, together)].reshape(together * cells, keyval.shape[2])
        scores = lax.dot_general(
            own, block, (((1,), (1,)), ((), ())), preferred_element_type=jnp.float32
        )
        return block, scores

    def attend(index):
        own = queries[index]
        if together == n_rows:
            block, scores = absorb(own, 0)
            row_max = jnp.max(scores, axis=-1, keepdims=True)
            weights = jnp.exp((scores - row_max) * scale)
            denominator = jnp.sum(weights, axis=-1, keepdims=True)
            weighted = jnp.dot(weights.astype(jnp.bfloat16), block, preferred_element_type=jnp.float32)
        else:

            def body(step, state):
                row_max, denominator, weighted = state
                block, scores = absorb(own, step)
                new_max = jnp.maximum(row_max, jnp.max(scores, axis=-1, keepdims=True))
                factor = jnp.exp((row_max - new_max) * scale)
                weights = jnp.exp((scores - new_max) * scale)
                return (
                    new_max,
                    denominator * factor + jnp.sum(weights, axis=-1, keepdims=True),
                    weighted * factor
                    + jnp.dot(weights.astype(jnp.bfloat16), block, preferred_element_type=jnp.float32),
                )

            initial = (
                jnp.full((pair, 1), -1e30, jnp.float32),
                jnp.zeros((pair, 1), jnp.float32),
                jnp.zeros((pair, 2 * head_size), jnp.float32),
            )
            row_max, denominator, weighted = lax.fori_loop(0, n_rows // together, body, initial)
        return (weighted[:, head_size:] / denominator).astype(jnp.bfloat16)

    def att_copy(target, step):
        return pltpu.make_async_remote_copy(
            src_ref=attention.at[0, target], dst_ref=attention.at[1, col],
            send_sem=att_send.at[step], recv_sem=att_recv.at[step],
            device_id={"cols": target}, device_id_type=MESH,
        )

    def serve(step):
        other = lax.rem(chip + step + 1, chips)
        found = attend(other)
        for which in range(cores):
            target = other * cores + lax.rem(core + which, cores)
            attention[0, other * cores + which] = found[which * strip : (which + 1) * strip]
        for which in range(cores):
            target = other * cores + lax.rem(core + which, cores)
            att_copy(target, (step + 1) * cores + which).start()

    repeat(chips - 1, serve)
    found = attend(chip)
    for which in range(cores):
        attention[0, chip * cores + which] = found[which * strip : (which + 1) * strip]
    if cores > 1:
        att_copy(sibling, 1).start()
    attention[1, col] = attention[0, col]

    for load in loads[5:]:
        load.wait()
    if cores > 1:
        att_copy(sibling, 1).wait_recv()
    for step in range(cores, n_cols):
        att_copy(sibling, step).wait_recv()
    together_heads = jnp.concatenate([attention[1, head] for head in range(n_cols)], axis=1)
    result = jnp.dot(together_heads, w_out[...], preferred_element_type=jnp.float32)
    result = result + out_bias[...].reshape(1, channels) + hidden[...].astype(jnp.float32).reshape(strip, channels)
    out[...] = result.reshape(out.shape).astype(jnp.bfloat16)

    for part in range(PIECES):
        repeat(chips - 1, lambda step, part=part: strip_copy(step, part).wait_send())
        if cores > 1:
            repeat(chips, lambda step, part=part: relay_copy(step, part).wait_send())
    for half in range(HALVES):
        handed_on(0, half)
        if few:
            for distance in range(1, n_rows - 1):
                handed_on(distance, half)
        else:
            pl.loop(1, n_rows - 1)(lambda distance, half=half: handed_on(distance, half))
    for step in range(1, n_cols):
        att_copy(sibling, step).wait_send()


def write_back(out, fresh, out_hbm, fresh_hbm, store_sem):
    stores = [
        pltpu.make_async_copy(out, out_hbm, store_sem.at[0]),
        pltpu.make_async_copy(fresh, fresh_hbm, store_sem.at[1]),
    ]
    for store in stores:
        store.start()
    for store in stores:
        store.wait()


def shards(n_rows, n_cols, hidden, ln_gain, ln_bias, w_query, w_keyval, stale_keyval, w_out, out_bias):
    band_rows, strip_cols, channels = hidden.shape
    head_size = w_query.shape[1]
    full_cols = stale_keyval.shape[1]
    cells = band_rows * full_cols
    strip = band_rows * strip_cols
    cores = 2 if n_cols % 2 == 0 else 1
    chips = n_cols // cores
    bf16, f32 = jnp.bfloat16, jnp.float32
    near = pl.BlockSpec(memory_space=pltpu.VMEM)
    far = pl.BlockSpec(memory_space=pltpu.HBM)
    dma = pltpu.SemaphoreType.DMA
    operands = (
        hidden,
        ln_gain,
        ln_bias,
        w_query.T,
        w_keyval,
        stale_keyval.reshape(cells, 2 * head_size),
        w_out,
        out_bias,
    )
    shapes = (hidden.shape, (band_rows, full_cols, 2 * head_size))
    found = pl.pallas_call(
        functools.partial(kernel, n_rows, n_cols, cores),
        out_shape=tuple(pltpu.VMEM(shape, bf16) for shape in shapes),
        in_specs=[far] * 8,
        out_specs=(near, near),
        scratch_shapes=[
            pltpu.VMEM(hidden.shape, bf16),
            pltpu.VMEM((channels,), f32),
            pltpu.VMEM((channels,), f32),
            pltpu.VMEM((channels,), f32),
            pltpu.VMEM((head_size, channels), bf16),
            pltpu.VMEM(w_keyval.shape, bf16),
            pltpu.VMEM(w_out.shape, bf16),
            pltpu.VMEM((chips, cores * strip, channels), bf16),
            pltpu.VMEM((chips, cores * strip, 2 * head_size), bf16),
            pltpu.VMEM((n_rows, cells, 2 * head_size), bf16),
            pltpu.VMEM((band_rows, n_cols, strip_cols, 2 * head_size), f32),
            pltpu.VMEM((2, n_cols, strip, head_size), bf16),
            dma((7,)),
            dma((n_rows, HALVES)),
            dma((n_rows, HALVES)),
            dma((n_rows, HALVES)),
            dma((n_rows, HALVES)),
            dma((chips, PIECES)),
            dma((chips, PIECES)),
            dma((chips, PIECES)),
            dma((chips, PIECES)),
            dma((n_cols,)),
            dma((n_cols,)),
        ],
        compiler_params=pltpu.CompilerParams(
            collective_id=0, has_side_effects=True, vmem_limit_bytes=48 * 1024 * 1024
        ),
    )(*(pltpu.with_memory_space_constraint(operand, pltpu.HBM) for operand in operands))
    out, fresh = pl.pallas_call(
        write_back,
        out_shape=tuple(pltpu.HBM(shape, bf16) for shape in shapes),
        in_specs=[pl.BlockSpec(memory_space=pl.ANY)] * 2,
        out_specs=(far, far),
        scratch_shapes=[dma((2,))],
        compiler_params=pltpu.CompilerParams(vmem_limit_bytes=2 * 1024 * 1024),
    )(*found)
    return out, fresh.reshape(band_rows, full_cols, 1, 2 * head_size)


def solution(mesh):
    return jax.shard_map(
        functools.partial(shards, mesh.shape["rows"], mesh.shape["cols"]),
        mesh=mesh,
        in_specs=(
            P(("groups", "rows"), "cols", None),
            P(),
            P(),
            P(None, "cols"),
            P(None, "cols"),
            P(("groups", "rows"), None, "cols", None),
            P(),
            P(),
        ),
        out_specs=(P(("groups", "rows"), "cols", None), P(("groups", "rows"), None, "cols", None)),
        check_vma=False,
    )
```

```python
import functools
import math

import jax
import jax.numpy as jnp
from jax import lax
from jax.experimental import pallas as pl
from jax.experimental.pallas import tpu as pltpu
from jax.sharding import PartitionSpec as P

MESH = pl.DeviceIdType.MESH
PIECES = 4


def repeat(count, body):
    if count <= 4:
        for index in range(count):
            body(index)
    else:
        lax.fori_loop(0, count, lambda index, carry: (body(index), carry)[1], 0)


def kernel(
    n_rows, n_cols, cores,
    hidden_hbm, gain_hbm, bias_hbm, w_query_hbm, w_keyval_hbm, stale_hbm, w_out_hbm, out_bias_hbm,
    out, fresh,
    hidden, gain, bias, out_bias, w_query, w_keyval, w_out, normed, queries, keyval, fresh_wide, attention,
    load_sem, band_send, band_recv, strip_send, strip_recv, relay_send, relay_recv, att_send, att_recv,
):
    row = lax.axis_index("rows")
    col = lax.axis_index("cols")
    chips = n_cols // cores
    chip, core = col // cores, col % cores
    sibling = chip * cores + (cores - 1 - core)
    band_rows, strip_cols, channels = hidden.shape
    strip = band_rows * strip_cols
    pair = cores * strip
    head_size = w_query.shape[0]
    piece = strip // PIECES
    scale = math.log2(math.e) / math.sqrt(head_size)

    loads = [
        pltpu.make_async_copy(source, target, load_sem.at[index])
        for index, (source, target) in enumerate(
            [
                (hidden_hbm, hidden),
                (gain_hbm, gain),
                (bias_hbm, bias),
                (w_query_hbm, w_query),
                (w_keyval_hbm, w_keyval),
                (w_out_hbm, w_out),
                (out_bias_hbm, out_bias),
            ]
        )
    ]
    for load in loads:
        load.start()

    barrier = pltpu.get_barrier_semaphore()

    def greet_col(step):
        pl.semaphore_signal(
            barrier, inc=1, device_id={"cols": lax.rem(col + step + 1, n_cols)}, device_id_type=MESH
        )

    def greet_row(step):
        pl.semaphore_signal(
            barrier, inc=1, device_id={"rows": lax.rem(row + step + 1, n_rows)}, device_id_type=MESH
        )

    repeat(n_cols - 1, greet_col)
    repeat(n_rows - 1, greet_row)

    def rows_of(core_index, part):
        return pl.ds(pl.multiple_of(core_index * strip + part * piece, piece), piece)

    def strip_copy(step, part):
        other = lax.rem(chip + step + 1, chips)
        block = normed.at[chip, rows_of(core, part), :]
        return pltpu.make_async_remote_copy(
            src_ref=block, dst_ref=block,
            send_sem=strip_send.at[step, part], recv_sem=strip_recv.at[step, part],
            device_id={"cols": other * cores + core}, device_id_type=MESH,
        )

    def relay_copy(step, part):
        source_chip = lax.rem(chip + chips - step, chips)
        block = normed.at[source_chip, rows_of(core, part), :]
        return pltpu.make_async_remote_copy(
            src_ref=block, dst_ref=block,
            send_sem=relay_send.at[step, part], recv_sem=relay_recv.at[step, part],
            device_id={"cols": sibling}, device_id_type=MESH,
        )

    def by_distance(step):
        tables = [sorted(range(n_rows), key=lambda band: (abs(band - at), band))[step] for at in range(n_rows)]
        band = tables[0]
        for at in range(1, n_rows):
            band = jnp.where(row == at, tables[at], band)
        return band

    def band_copy(target):
        return pltpu.make_async_remote_copy(
            src_ref=stale_hbm, dst_ref=keyval.at[row],
            send_sem=band_send.at[target], recv_sem=band_recv.at[row],
            device_id={"rows": target}, device_id_type=MESH,
        )

    def band_arrived(band):
        pltpu.make_async_copy(keyval.at[band], keyval.at[band], band_recv.at[band]).wait()

    pl.semaphore_wait(barrier, n_cols - 1 + n_rows - 1)
    for step in range(1, n_rows):
        band_copy(by_distance(step)).start()

    for load in loads[:3]:
        load.wait()
    gains, biases = gain[...].reshape(1, channels), bias[...].reshape(1, channels)
    piece_rows = band_rows // PIECES
    for part in range(PIECES):
        values = hidden[part * piece_rows : (part + 1) * piece_rows].astype(jnp.float32)
        values = values.reshape(piece, channels)
        centred = values - jnp.mean(values, axis=-1, keepdims=True)
        variance = jnp.mean(centred * centred, axis=-1, keepdims=True)
        normed[chip, rows_of(core, part), :] = (
            centred * lax.rsqrt(variance + 1e-05) * gains + biases
        ).astype(jnp.bfloat16)
        repeat(chips - 1, lambda step: strip_copy(step, part).start())
        if cores > 1:
            relay_copy(0, part).start()

    def project(index):
        rows = normed[index]
        own = lax.dot_general(
            rows, w_query[...], (((1,), (1,)), ((), ())), preferred_element_type=jnp.float32
        ).astype(jnp.bfloat16)
        queries[index] = jnp.concatenate([own, jnp.zeros_like(own)], axis=1)
        both = jnp.dot(rows, w_keyval[...], preferred_element_type=jnp.float32).astype(jnp.bfloat16)
        keyval[row, pl.ds(pl.multiple_of(index * pair, pair), pair), :] = both
        wide = both.astype(jnp.float32).reshape(cores, band_rows, strip_cols, both.shape[1])
        for which in range(cores):
            fresh_wide[:, index * cores + which] = wide[which]

    for load in loads[3:5]:
        load.wait()
    if cores > 1:
        for part in range(PIECES):
            relay_copy(0, part).wait_recv()
    project(chip)

    def arrive(step):
        for part in range(PIECES):
            strip_copy(step, part).wait_recv()
            if cores > 1:
                relay_copy(step + 1, part).start()
        if cores > 1:
            for part in range(PIECES):
                relay_copy(step + 1, part).wait_recv()
        project(lax.rem(chip + chips - step - 1, chips))

    repeat(chips - 1, arrive)

    fresh[...] = fresh_wide[...].reshape(fresh.shape).astype(jnp.bfloat16)

    def absorb(state, own, band):
        block = keyval[band]
        scores = lax.dot_general(
            own, block, (((1,), (1,)), ((), ())), preferred_element_type=jnp.float32
        )
        new_max = jnp.max(scores, axis=-1, keepdims=True)
        if state is not None:
            new_max = jnp.maximum(state[0], new_max)
        weights = jnp.exp2((scores - new_max) * scale)
        denominator = jnp.sum(weights, axis=-1, keepdims=True)
        weighted = jnp.dot(weights.astype(jnp.bfloat16), block, preferred_element_type=jnp.float32)
        if state is not None:
            factor = jnp.exp2((state[0] - new_max) * scale)
            denominator = state[1] * factor + denominator
            weighted = state[2] * factor + weighted
        return new_max, denominator, weighted

    def keep(state, first, count):
        found = (state[2][:, head_size:] / state[1]).astype(jnp.bfloat16)
        for which in range(count):
            attention[0, first + which] = found[which * strip : (which + 1) * strip]

    if n_rows * chips <= 16:
        own = queries[...].reshape(n_cols * strip, queries.shape[2])
        state = absorb(None, own, row)
        for step in range(1, n_rows):
            band = by_distance(step)
            band_arrived(band)
            state = absorb(state, own, band)
        keep(state, 0, n_cols)
    else:
        for step in range(1, n_rows):
            band_arrived(by_distance(step))

        @pl.loop(0, chips)
        def each_pair(index):
            own = queries[index]
            state = lax.fori_loop(1, n_rows, lambda band, state: absorb(state, own, band), absorb(None, own, 0))
            keep(state, index * cores, cores)

    def att_copy(target, step):
        return pltpu.make_async_remote_copy(
            src_ref=attention.at[0, target], dst_ref=attention.at[1, col],
            send_sem=att_send.at[step], recv_sem=att_recv.at[step],
            device_id={"cols": target}, device_id_type=MESH,
        )

    def serve(step):
        other = lax.rem(chip + step + 1, chips)
        for which in range(cores):
            target = other * cores + lax.rem(core + which, cores)
            att_copy(target, (step + 1) * cores + which).start()

    repeat(chips - 1, serve)
    if cores > 1:
        att_copy(sibling, 1).start()
    attention[1, col] = attention[0, col]

    for load in loads[5:]:
        load.wait()
    if cores > 1:
        att_copy(sibling, 1).wait_recv()
    for step in range(cores, n_cols):
        att_copy(sibling, step).wait_recv()
    together_heads = jnp.concatenate([attention[1, head] for head in range(n_cols)], axis=1)
    result = jnp.dot(together_heads, w_out[...], preferred_element_type=jnp.float32)
    result = result + out_bias[...].reshape(1, channels) + hidden[...].astype(jnp.float32).reshape(strip, channels)
    out[...] = result.reshape(out.shape).astype(jnp.bfloat16)

    for part in range(PIECES):
        repeat(chips - 1, lambda step, part=part: strip_copy(step, part).wait_send())
        if cores > 1:
            repeat(chips, lambda step, part=part: relay_copy(step, part).wait_send())
    for step in range(1, n_rows):
        band_copy(by_distance(step)).wait_send()
    for step in range(1, n_cols):
        att_copy(sibling, step).wait_send()


def write_back(out, fresh, out_hbm, fresh_hbm, store_sem):
    stores = [
        pltpu.make_async_copy(out, out_hbm, store_sem.at[0]),
        pltpu.make_async_copy(fresh, fresh_hbm, store_sem.at[1]),
    ]
    for store in stores:
        store.start()
    for store in stores:
        store.wait()


def shards(n_rows, n_cols, hidden, ln_gain, ln_bias, w_query, w_keyval, stale_keyval, w_out, out_bias):
    band_rows, strip_cols, channels = hidden.shape
    head_size = w_query.shape[1]
    full_cols = stale_keyval.shape[1]
    cells = band_rows * full_cols
    strip = band_rows * strip_cols
    cores = 2 if n_cols % 2 == 0 else 1
    chips = n_cols // cores
    bf16, f32 = jnp.bfloat16, jnp.float32
    near = pl.BlockSpec(memory_space=pltpu.VMEM)
    far = pl.BlockSpec(memory_space=pltpu.HBM)
    dma = pltpu.SemaphoreType.DMA
    operands = (
        hidden,
        ln_gain,
        ln_bias,
        w_query.T,
        w_keyval,
        stale_keyval.reshape(cells, 2 * head_size),
        w_out,
        out_bias,
    )
    shapes = (hidden.shape, (band_rows, full_cols, 2 * head_size))
    found = pl.pallas_call(
        functools.partial(kernel, n_rows, n_cols, cores),
        out_shape=tuple(pltpu.VMEM(shape, bf16) for shape in shapes),
        in_specs=[far] * 8,
        out_specs=(near, near),
        scratch_shapes=[
            pltpu.VMEM(hidden.shape, bf16),
            pltpu.VMEM((channels,), f32),
            pltpu.VMEM((channels,), f32),
            pltpu.VMEM((channels,), f32),
            pltpu.VMEM((head_size, channels), bf16),
            pltpu.VMEM(w_keyval.shape, bf16),
            pltpu.VMEM(w_out.shape, bf16),
            pltpu.VMEM((chips, cores * strip, channels), bf16),
            pltpu.VMEM((chips, cores * strip, 2 * head_size), bf16),
            pltpu.VMEM((n_rows, cells, 2 * head_size), bf16),
            pltpu.VMEM((band_rows, n_cols, strip_cols, 2 * head_size), f32),
            pltpu.VMEM((2, n_cols, strip, head_size), bf16),
            dma((7,)),
            dma((n_rows,)),
            dma((n_rows,)),
            dma((chips, PIECES)),
            dma((chips, PIECES)),
            dma((chips, PIECES)),
            dma((chips, PIECES)),
            dma((n_cols,)),
            dma((n_cols,)),
        ],
        compiler_params=pltpu.CompilerParams(
            collective_id=0, has_side_effects=True, vmem_limit_bytes=48 * 1024 * 1024
        ),
    )(*(pltpu.with_memory_space_constraint(operand, pltpu.HBM) for operand in operands))
    out, fresh = pl.pallas_call(
        write_back,
        out_shape=tuple(pltpu.HBM(shape, bf16) for shape in shapes),
        in_specs=[pl.BlockSpec(memory_space=pl.ANY)] * 2,
        out_specs=(far, far),
        scratch_shapes=[dma((2,))],
        compiler_params=pltpu.CompilerParams(vmem_limit_bytes=2 * 1024 * 1024),
    )(*found)
    return out, fresh.reshape(band_rows, full_cols, 1, 2 * head_size)


def solution(mesh):
    return jax.shard_map(
        functools.partial(shards, mesh.shape["rows"], mesh.shape["cols"]),
        mesh=mesh,
        in_specs=(
            P(("groups", "rows"), "cols", None),
            P(),
            P(),
            P(None, "cols"),
            P(None, "cols"),
            P(("groups", "rows"), None, "cols", None),
            P(),
            P(),
        ),
        out_specs=(P(("groups", "rows"), "cols", None), P(("groups", "rows"), None, "cols", None)),
        check_vma=False,
    )
```

```python
import functools
import math

import jax
import jax.numpy as jnp
from jax import lax
from jax.experimental import pallas as pl
from jax.experimental.pallas import tpu as pltpu
from jax.sharding import PartitionSpec as P

MESH = pl.DeviceIdType.MESH
PIECES = 4


def repeat(count, body):
    if count <= 4:
        for index in range(count):
            body(index)
    else:
        lax.fori_loop(0, count, lambda index, carry: (body(index), carry)[1], 0)


def kernel(
    n_rows, n_cols, cores,
    hidden_hbm, gain_hbm, bias_hbm, w_query_hbm, w_keyval_hbm, stale_hbm, w_out_hbm, out_bias_hbm,
    out, fresh,
    hidden, gain, bias, out_bias, w_query, w_keyval, w_out, normed, queries, keyval, fresh_wide, attention,
    load_sem, band_send, band_recv, strip_send, strip_recv, relay_send, relay_recv, att_send, att_recv,
):
    row = lax.axis_index("rows")
    col = lax.axis_index("cols")
    chips = n_cols // cores
    chip, core = col // cores, col % cores
    sibling = chip * cores + (cores - 1 - core)
    band_rows, strip_cols, channels = hidden.shape
    strip = band_rows * strip_cols
    pair = cores * strip
    head_size = w_query.shape[0]
    piece = strip // PIECES
    scale = math.log2(math.e) / math.sqrt(head_size)

    loads = [
        pltpu.make_async_copy(source, target, load_sem.at[index])
        for index, (source, target) in enumerate(
            [
                (hidden_hbm, hidden),
                (gain_hbm, gain),
                (bias_hbm, bias),
                (w_query_hbm, w_query),
                (w_keyval_hbm, w_keyval),
                (w_out_hbm, w_out),
                (out_bias_hbm, out_bias),
            ]
        )
    ]
    for load in loads:
        load.start()

    barrier = pltpu.get_barrier_semaphore()

    def greet_col(step):
        pl.semaphore_signal(
            barrier, inc=1, device_id={"cols": lax.rem(col + step + 1, n_cols)}, device_id_type=MESH
        )

    def greet_row(step):
        pl.semaphore_signal(
            barrier, inc=1, device_id={"rows": lax.rem(row + step + 1, n_rows)}, device_id_type=MESH
        )

    repeat(n_cols - 1, greet_col)
    repeat(n_rows - 1, greet_row)

    def rows_of(core_index, part):
        return pl.ds(pl.multiple_of(core_index * strip + part * piece, piece), piece)

    def strip_copy(step, part):
        other = lax.rem(chip + step + 1, chips)
        block = normed.at[chip, rows_of(core, part), :]
        return pltpu.make_async_remote_copy(
            src_ref=block, dst_ref=block,
            send_sem=strip_send.at[step, part], recv_sem=strip_recv.at[step, part],
            device_id={"cols": other * cores + core}, device_id_type=MESH,
        )

    def relay_copy(step, part):
        source_chip = lax.rem(chip + chips - step, chips)
        block = normed.at[source_chip, rows_of(core, part), :]
        return pltpu.make_async_remote_copy(
            src_ref=block, dst_ref=block,
            send_sem=relay_send.at[step, part], recv_sem=relay_recv.at[step, part],
            device_id={"cols": sibling}, device_id_type=MESH,
        )

    def by_distance(step):
        tables = [sorted(range(n_rows), key=lambda band: (abs(band - at), band))[step] for at in range(n_rows)]
        band = tables[0]
        for at in range(1, n_rows):
            band = jnp.where(row == at, tables[at], band)
        return band

    def band_copy(target):
        return pltpu.make_async_remote_copy(
            src_ref=stale_hbm, dst_ref=keyval.at[row],
            send_sem=band_send.at[target], recv_sem=band_recv.at[row],
            device_id={"rows": target}, device_id_type=MESH,
        )

    def band_arrived(band):
        pltpu.make_async_copy(keyval.at[band], keyval.at[band], band_recv.at[band]).wait()

    pl.semaphore_wait(barrier, n_cols - 1 + n_rows - 1)
    for step in range(1, n_rows):
        band_copy(by_distance(step)).start()

    for load in loads[:3]:
        load.wait()
    gains, biases = gain[...].reshape(1, channels), bias[...].reshape(1, channels)
    piece_rows = band_rows // PIECES
    for part in range(PIECES):
        values = hidden[part * piece_rows : (part + 1) * piece_rows].astype(jnp.float32)
        values = values.reshape(piece, channels)
        centred = values - jnp.mean(values, axis=-1, keepdims=True)
        variance = jnp.mean(centred * centred, axis=-1, keepdims=True)
        normed[chip, rows_of(core, part), :] = (
            centred * lax.rsqrt(variance + 1e-05) * gains + biases
        ).astype(jnp.bfloat16)
        repeat(chips - 1, lambda step: strip_copy(step, part).start())
        if cores > 1:
            relay_copy(0, part).start()

    def project(index):
        rows = normed[index]
        own = lax.dot_general(
            rows, w_query[...], (((1,), (1,)), ((), ())), preferred_element_type=jnp.float32
        ).astype(jnp.bfloat16)
        queries[index] = jnp.concatenate([own, jnp.zeros_like(own)], axis=1)
        both = jnp.dot(rows, w_keyval[...], preferred_element_type=jnp.float32).astype(jnp.bfloat16)
        keyval[row, pl.ds(pl.multiple_of(index * pair, pair), pair), :] = both
        wide = both.astype(jnp.float32).reshape(cores, band_rows, strip_cols, both.shape[1])
        for which in range(cores):
            fresh_wide[:, index * cores + which] = wide[which]

    for load in loads[3:5]:
        load.wait()
    if cores > 1:
        for part in range(PIECES):
            relay_copy(0, part).wait_recv()
    project(chip)

    def arrive(step):
        for part in range(PIECES):
            strip_copy(step, part).wait_recv()
            if cores > 1:
                relay_copy(step + 1, part).start()
        if cores > 1:
            for part in range(PIECES):
                relay_copy(step + 1, part).wait_recv()
        project(lax.rem(chip + chips - step - 1, chips))

    repeat(chips - 1, arrive)

    fresh[...] = fresh_wide[...].reshape(fresh.shape).astype(jnp.bfloat16)

    def absorb(state, own, band):
        block = keyval[band]
        scores = lax.dot_general(
            block, own, (((1,), (1,)), ((), ())), preferred_element_type=jnp.float32
        )
        block_values = block.T[head_size:]
        new_max = jnp.max(scores, axis=0, keepdims=True)
        if state is not None:
            new_max = jnp.maximum(state[0], new_max)
        weights = jnp.exp2((scores - new_max) * scale)
        denominator = jnp.sum(weights, axis=0, keepdims=True)
        weighted = jnp.dot(block_values, weights.astype(jnp.bfloat16), preferred_element_type=jnp.float32)
        if state is not None:
            factor = jnp.exp2((state[0] - new_max) * scale)
            denominator = state[1] * factor + denominator
            weighted = state[2] * factor + weighted
        return new_max, denominator, weighted

    def keep(state, first, count):
        found = (state[2] / state[1]).T.astype(jnp.bfloat16)
        for which in range(count):
            attention[0, first + which] = found[which * strip : (which + 1) * strip]

    if n_rows * chips <= 16:
        own = queries[...].reshape(n_cols * strip, queries.shape[2])
        state = absorb(None, own, row)
        for step in range(1, n_rows):
            band = by_distance(step)
            band_arrived(band)
            state = absorb(state, own, band)
        keep(state, 0, n_cols)
    else:
        for step in range(1, n_rows):
            band_arrived(by_distance(step))

        @pl.loop(0, chips)
        def each_pair(index):
            own = queries[index]
            state = lax.fori_loop(1, n_rows, lambda band, state: absorb(state, own, band), absorb(None, own, 0))
            keep(state, index * cores, cores)

    def att_copy(target, step):
        return pltpu.make_async_remote_copy(
            src_ref=attention.at[0, target], dst_ref=attention.at[1, col],
            send_sem=att_send.at[step], recv_sem=att_recv.at[step],
            device_id={"cols": target}, device_id_type=MESH,
        )

    def serve(step):
        other = lax.rem(chip + step + 1, chips)
        for which in range(cores):
            target = other * cores + lax.rem(core + which, cores)
            att_copy(target, (step + 1) * cores + which).start()

    repeat(chips - 1, serve)
    if cores > 1:
        att_copy(sibling, 1).start()
    attention[1, col] = attention[0, col]

    for load in loads[5:]:
        load.wait()
    if cores > 1:
        att_copy(sibling, 1).wait_recv()
    for step in range(cores, n_cols):
        att_copy(sibling, step).wait_recv()
    together_heads = jnp.concatenate([attention[1, head] for head in range(n_cols)], axis=1)
    result = jnp.dot(together_heads, w_out[...], preferred_element_type=jnp.float32)
    result = result + out_bias[...].reshape(1, channels) + hidden[...].astype(jnp.float32).reshape(strip, channels)
    out[...] = result.reshape(out.shape).astype(jnp.bfloat16)

    for part in range(PIECES):
        repeat(chips - 1, lambda step, part=part: strip_copy(step, part).wait_send())
        if cores > 1:
            repeat(chips, lambda step, part=part: relay_copy(step, part).wait_send())
    for step in range(1, n_rows):
        band_copy(by_distance(step)).wait_send()
    for step in range(1, n_cols):
        att_copy(sibling, step).wait_send()


def write_back(out, fresh, out_hbm, fresh_hbm, store_sem):
    stores = [
        pltpu.make_async_copy(out, out_hbm, store_sem.at[0]),
        pltpu.make_async_copy(fresh, fresh_hbm, store_sem.at[1]),
    ]
    for store in stores:
        store.start()
    for store in stores:
        store.wait()


def shards(n_rows, n_cols, hidden, ln_gain, ln_bias, w_query, w_keyval, stale_keyval, w_out, out_bias):
    band_rows, strip_cols, channels = hidden.shape
    head_size = w_query.shape[1]
    full_cols = stale_keyval.shape[1]
    cells = band_rows * full_cols
    strip = band_rows * strip_cols
    cores = 2 if n_cols % 2 == 0 else 1
    chips = n_cols // cores
    bf16, f32 = jnp.bfloat16, jnp.float32
    near = pl.BlockSpec(memory_space=pltpu.VMEM)
    far = pl.BlockSpec(memory_space=pltpu.HBM)
    dma = pltpu.SemaphoreType.DMA
    operands = (
        hidden,
        ln_gain,
        ln_bias,
        w_query.T,
        w_keyval,
        stale_keyval.reshape(cells, 2 * head_size),
        w_out,
        out_bias,
    )
    shapes = (hidden.shape, (band_rows, full_cols, 2 * head_size))
    found = pl.pallas_call(
        functools.partial(kernel, n_rows, n_cols, cores),
        out_shape=tuple(pltpu.VMEM(shape, bf16) for shape in shapes),
        in_specs=[far] * 8,
        out_specs=(near, near),
        scratch_shapes=[
            pltpu.VMEM(hidden.shape, bf16),
            pltpu.VMEM((channels,), f32),
            pltpu.VMEM((channels,), f32),
            pltpu.VMEM((channels,), f32),
            pltpu.VMEM((head_size, channels), bf16),
            pltpu.VMEM(w_keyval.shape, bf16),
            pltpu.VMEM(w_out.shape, bf16),
            pltpu.VMEM((chips, cores * strip, channels), bf16),
            pltpu.VMEM((chips, cores * strip, 2 * head_size), bf16),
            pltpu.VMEM((n_rows, cells, 2 * head_size), bf16),
            pltpu.VMEM((band_rows, n_cols, strip_cols, 2 * head_size), f32),
            pltpu.VMEM((2, n_cols, strip, head_size), bf16),
            dma((7,)),
            dma((n_rows,)),
            dma((n_rows,)),
            dma((chips, PIECES)),
            dma((chips, PIECES)),
            dma((chips, PIECES)),
            dma((chips, PIECES)),
            dma((n_cols,)),
            dma((n_cols,)),
        ],
        compiler_params=pltpu.CompilerParams(
            collective_id=0, has_side_effects=True, vmem_limit_bytes=48 * 1024 * 1024
        ),
    )(*(pltpu.with_memory_space_constraint(operand, pltpu.HBM) for operand in operands))
    out, fresh = pl.pallas_call(
        write_back,
        out_shape=tuple(pltpu.HBM(shape, bf16) for shape in shapes),
        in_specs=[pl.BlockSpec(memory_space=pl.ANY)] * 2,
        out_specs=(far, far),
        scratch_shapes=[dma((2,))],
        compiler_params=pltpu.CompilerParams(vmem_limit_bytes=2 * 1024 * 1024),
    )(*found)
    return out, fresh.reshape(band_rows, full_cols, 1, 2 * head_size)


def solution(mesh):
    return jax.shard_map(
        functools.partial(shards, mesh.shape["rows"], mesh.shape["cols"]),
        mesh=mesh,
        in_specs=(
            P(("groups", "rows"), "cols", None),
            P(),
            P(),
            P(None, "cols"),
            P(None, "cols"),
            P(("groups", "rows"), None, "cols", None),
            P(),
            P(),
        ),
        out_specs=(P(("groups", "rows"), "cols", None), P(("groups", "rows"), None, "cols", None)),
        check_vma=False,
    )
```

```python
import functools
import math

import jax
import jax.numpy as jnp
from jax import lax
from jax.experimental import pallas as pl
from jax.experimental.pallas import tpu as pltpu
from jax.sharding import PartitionSpec as P

MESH = pl.DeviceIdType.MESH
PIECES = 4


def repeat(count, body):
    if count <= 4:
        for index in range(count):
            body(index)
    else:
        lax.fori_loop(0, count, lambda index, carry: (body(index), carry)[1], 0)


def kernel(
    n_rows, n_cols, cores,
    hidden_hbm, gain_hbm, bias_hbm, w_query_hbm, w_keyval_hbm, stale_hbm, w_out_hbm, out_bias_hbm,
    out, fresh,
    hidden, gain, bias, out_bias, w_query, w_keyval, w_out, normed, queries, keyval, fresh_wide, attention,
    load_sem, band_send, band_recv, strip_send, strip_recv, relay_send, relay_recv, att_send, att_recv,
):
    row = lax.axis_index("rows")
    col = lax.axis_index("cols")
    chips = n_cols // cores
    chip, core = col // cores, col % cores
    sibling = chip * cores + (cores - 1 - core)
    band_rows, strip_cols, channels = hidden.shape
    strip = band_rows * strip_cols
    pair = cores * strip
    head_size = w_query.shape[0]
    piece = strip // PIECES
    scale = math.log2(math.e) / math.sqrt(head_size)

    loads = [
        pltpu.make_async_copy(source, target, load_sem.at[index])
        for index, (source, target) in enumerate(
            [
                (hidden_hbm, hidden),
                (gain_hbm, gain),
                (bias_hbm, bias),
                (w_query_hbm, w_query),
                (w_keyval_hbm, w_keyval),
                (w_out_hbm, w_out),
                (out_bias_hbm, out_bias),
            ]
        )
    ]
    for load in loads:
        load.start()

    barrier = pltpu.get_barrier_semaphore()

    def greet_col(step):
        pl.semaphore_signal(
            barrier, inc=1, device_id={"cols": lax.rem(col + step + 1, n_cols)}, device_id_type=MESH
        )

    def greet_row(step):
        pl.semaphore_signal(
            barrier, inc=1, device_id={"rows": lax.rem(row + step + 1, n_rows)}, device_id_type=MESH
        )

    repeat(n_cols - 1, greet_col)
    repeat(n_rows - 1, greet_row)

    def rows_of(core_index, part):
        return pl.ds(pl.multiple_of(core_index * strip + part * piece, piece), piece)

    def strip_copy(step, part):
        other = lax.rem(chip + step + 1, chips)
        block = normed.at[chip, rows_of(core, part), :]
        return pltpu.make_async_remote_copy(
            src_ref=block, dst_ref=block,
            send_sem=strip_send.at[step, part], recv_sem=strip_recv.at[step, part],
            device_id={"cols": other * cores + core}, device_id_type=MESH,
        )

    def relay_copy(step, part):
        source_chip = lax.rem(chip + chips - step, chips)
        block = normed.at[source_chip, rows_of(core, part), :]
        return pltpu.make_async_remote_copy(
            src_ref=block, dst_ref=block,
            send_sem=relay_send.at[step, part], recv_sem=relay_recv.at[step, part],
            device_id={"cols": sibling}, device_id_type=MESH,
        )

    def by_distance(step):
        tables = [sorted(range(n_rows), key=lambda band: (abs(band - at), band))[step] for at in range(n_rows)]
        band = tables[0]
        for at in range(1, n_rows):
            band = jnp.where(row == at, tables[at], band)
        return band

    def band_copy(target):
        return pltpu.make_async_remote_copy(
            src_ref=stale_hbm, dst_ref=keyval.at[row],
            send_sem=band_send.at[target], recv_sem=band_recv.at[row],
            device_id={"rows": target}, device_id_type=MESH,
        )

    def band_arrived(band):
        pltpu.make_async_copy(keyval.at[band], keyval.at[band], band_recv.at[band]).wait()

    pl.semaphore_wait(barrier, n_cols - 1 + n_rows - 1)
    for step in range(1, n_rows):
        band_copy(by_distance(n_rows - step)).start()

    for load in loads[:3]:
        load.wait()
    gains, biases = gain[...].reshape(1, channels), bias[...].reshape(1, channels)
    piece_rows = band_rows // PIECES
    for part in range(PIECES):
        values = hidden[part * piece_rows : (part + 1) * piece_rows].astype(jnp.float32)
        values = values.reshape(piece, channels)
        centred = values - jnp.mean(values, axis=-1, keepdims=True)
        variance = jnp.mean(centred * centred, axis=-1, keepdims=True)
        normed[chip, rows_of(core, part), :] = (
            centred * lax.rsqrt(variance + 1e-05) * gains + biases
        ).astype(jnp.bfloat16)
        repeat(chips - 1, lambda step: strip_copy(step, part).start())
        if cores > 1:
            relay_copy(0, part).start()

    def project(index):
        rows = normed[index]
        own = lax.dot_general(
            rows, w_query[...], (((1,), (1,)), ((), ())), preferred_element_type=jnp.float32
        ).astype(jnp.bfloat16)
        queries[index] = jnp.concatenate([own, jnp.zeros_like(own)], axis=1)
        both = jnp.dot(rows, w_keyval[...], preferred_element_type=jnp.float32).astype(jnp.bfloat16)
        keyval[row, pl.ds(pl.multiple_of(index * pair, pair), pair), :] = both
        wide = both.astype(jnp.float32).reshape(cores, band_rows, strip_cols, both.shape[1])
        for which in range(cores):
            fresh_wide[:, index * cores + which] = wide[which]

    for load in loads[3:5]:
        load.wait()
    if cores > 1:
        for part in range(PIECES):
            relay_copy(0, part).wait_recv()
    project(chip)

    def arrive(step):
        for part in range(PIECES):
            strip_copy(step, part).wait_recv()
            if cores > 1:
                relay_copy(step + 1, part).start()
        if cores > 1:
            for part in range(PIECES):
                relay_copy(step + 1, part).wait_recv()
        project(lax.rem(chip + chips - step - 1, chips))

    repeat(chips - 1, arrive)

    fresh[...] = fresh_wide[...].reshape(fresh.shape).astype(jnp.bfloat16)

    cells = keyval.shape[1]
    together = max(size for size in range(1, n_rows + 1) if n_rows % size == 0 and (size == 1 or size * cells <= 1024))

    def absorb(state, own, band):
        block = keyval[pl.ds(band * together, together)].reshape(together * cells, keyval.shape[2])
        scores = lax.dot_general(
            block, own, (((1,), (1,)), ((), ())), preferred_element_type=jnp.float32
        )
        block_values = block.T[head_size:]
        new_max = jnp.max(scores, axis=0, keepdims=True)
        if state is not None:
            new_max = jnp.maximum(state[0], new_max)
        weights = jnp.exp2((scores - new_max) * scale)
        denominator = jnp.sum(weights, axis=0, keepdims=True)
        weighted = jnp.dot(block_values, weights.astype(jnp.bfloat16), preferred_element_type=jnp.float32)
        if state is not None:
            factor = jnp.exp2((state[0] - new_max) * scale)
            denominator = state[1] * factor + denominator
            weighted = state[2] * factor + weighted
        return new_max, denominator, weighted

    def keep(state, first, count):
        found = (state[2] / state[1]).T.astype(jnp.bfloat16)
        for which in range(count):
            attention[0, first + which] = found[which * strip : (which + 1) * strip]

    def attend(index):
        own = queries[index]
        state = absorb(None, own, 0)
        if together < n_rows:
            state = lax.fori_loop(
                1, n_rows // together, lambda block, state: absorb(state, own, block), state
            )
        keep(state, index * cores, cores)

    for step in range(1, n_rows):
        band_arrived(by_distance(step))

    def att_copy(target, step):
        return pltpu.make_async_remote_copy(
            src_ref=attention.at[0, target], dst_ref=attention.at[1, col],
            send_sem=att_send.at[step], recv_sem=att_recv.at[step],
            device_id={"cols": target}, device_id_type=MESH,
        )

    def serve(step):
        other = lax.rem(chip + step + 1, chips)
        attend(other)
        for which in range(cores):
            target = other * cores + lax.rem(core + which, cores)
            att_copy(target, (step + 1) * cores + which).start()

    repeat(chips - 1, serve)
    attend(chip)
    if cores > 1:
        att_copy(sibling, 1).start()
    attention[1, col] = attention[0, col]

    for load in loads[5:]:
        load.wait()
    if cores > 1:
        att_copy(sibling, 1).wait_recv()
    for step in range(cores, n_cols):
        att_copy(sibling, step).wait_recv()
    together_heads = jnp.concatenate([attention[1, head] for head in range(n_cols)], axis=1)
    result = jnp.dot(together_heads, w_out[...], preferred_element_type=jnp.float32)
    result = result + out_bias[...].reshape(1, channels) + hidden[...].astype(jnp.float32).reshape(strip, channels)
    out[...] = result.reshape(out.shape).astype(jnp.bfloat16)

    for part in range(PIECES):
        repeat(chips - 1, lambda step, part=part: strip_copy(step, part).wait_send())
        if cores > 1:
            repeat(chips, lambda step, part=part: relay_copy(step, part).wait_send())
    for step in range(1, n_rows):
        band_copy(by_distance(step)).wait_send()
    for step in range(1, n_cols):
        att_copy(sibling, step).wait_send()


def write_back(out, fresh, out_hbm, fresh_hbm, store_sem):
    stores = [
        pltpu.make_async_copy(out, out_hbm, store_sem.at[0]),
        pltpu.make_async_copy(fresh, fresh_hbm, store_sem.at[1]),
    ]
    for store in stores:
        store.start()
    for store in stores:
        store.wait()


def shards(n_rows, n_cols, hidden, ln_gain, ln_bias, w_query, w_keyval, stale_keyval, w_out, out_bias):
    band_rows, strip_cols, channels = hidden.shape
    head_size = w_query.shape[1]
    full_cols = stale_keyval.shape[1]
    cells = band_rows * full_cols
    strip = band_rows * strip_cols
    cores = 2 if n_cols % 2 == 0 else 1
    chips = n_cols // cores
    bf16, f32 = jnp.bfloat16, jnp.float32
    near = pl.BlockSpec(memory_space=pltpu.VMEM)
    far = pl.BlockSpec(memory_space=pltpu.HBM)
    dma = pltpu.SemaphoreType.DMA
    operands = (
        hidden,
        ln_gain,
        ln_bias,
        w_query.T,
        w_keyval,
        stale_keyval.reshape(cells, 2 * head_size),
        w_out,
        out_bias,
    )
    shapes = (hidden.shape, (band_rows, full_cols, 2 * head_size))
    found = pl.pallas_call(
        functools.partial(kernel, n_rows, n_cols, cores),
        out_shape=tuple(pltpu.VMEM(shape, bf16) for shape in shapes),
        in_specs=[far] * 8,
        out_specs=(near, near),
        scratch_shapes=[
            pltpu.VMEM(hidden.shape, bf16),
            pltpu.VMEM((channels,), f32),
            pltpu.VMEM((channels,), f32),
            pltpu.VMEM((channels,), f32),
            pltpu.VMEM((head_size, channels), bf16),
            pltpu.VMEM(w_keyval.shape, bf16),
            pltpu.VMEM(w_out.shape, bf16),
            pltpu.VMEM((chips, cores * strip, channels), bf16),
            pltpu.VMEM((chips, cores * strip, 2 * head_size), bf16),
            pltpu.VMEM((n_rows, cells, 2 * head_size), bf16),
            pltpu.VMEM((band_rows, n_cols, strip_cols, 2 * head_size), f32),
            pltpu.VMEM((2, n_cols, strip, head_size), bf16),
            dma((7,)),
            dma((n_rows,)),
            dma((n_rows,)),
            dma((chips, PIECES)),
            dma((chips, PIECES)),
            dma((chips, PIECES)),
            dma((chips, PIECES)),
            dma((n_cols,)),
            dma((n_cols,)),
        ],
        compiler_params=pltpu.CompilerParams(
            collective_id=0, has_side_effects=True, vmem_limit_bytes=48 * 1024 * 1024
        ),
    )(*(pltpu.with_memory_space_constraint(operand, pltpu.HBM) for operand in operands))
    out, fresh = pl.pallas_call(
        write_back,
        out_shape=tuple(pltpu.HBM(shape, bf16) for shape in shapes),
        in_specs=[pl.BlockSpec(memory_space=pl.ANY)] * 2,
        out_specs=(far, far),
        scratch_shapes=[dma((2,))],
        compiler_params=pltpu.CompilerParams(vmem_limit_bytes=2 * 1024 * 1024),
    )(*found)
    return out, fresh.reshape(band_rows, full_cols, 1, 2 * head_size)


def solution(mesh):
    return jax.shard_map(
        functools.partial(shards, mesh.shape["rows"], mesh.shape["cols"]),
        mesh=mesh,
        in_specs=(
            P(("groups", "rows"), "cols", None),
            P(),
            P(),
            P(None, "cols"),
            P(None, "cols"),
            P(("groups", "rows"), None, "cols", None),
            P(),
            P(),
        ),
        out_specs=(P(("groups", "rows"), "cols", None), P(("groups", "rows"), None, "cols", None)),
        check_vma=False,
    )
```

```python
import functools
import math

import jax
import jax.numpy as jnp
from jax import lax
from jax.experimental import pallas as pl
from jax.experimental.pallas import tpu as pltpu
from jax.sharding import PartitionSpec as P

MESH = pl.DeviceIdType.MESH
PIECES = 4


def repeat(count, body):
    if count <= 4:
        for index in range(count):
            body(index)
    else:
        lax.fori_loop(0, count, lambda index, carry: (body(index), carry)[1], 0)


def kernel(
    n_rows, n_cols, cores,
    hidden_hbm, gain_hbm, bias_hbm, w_query_hbm, w_keyval_hbm, stale_hbm, w_out_hbm, out_bias_hbm,
    out, fresh,
    hidden, gain, bias, out_bias, w_query, w_keyval, w_out, normed, queries, keyval, fresh_wide, attention,
    load_sem, band_send, band_recv, strip_send, strip_recv, relay_send, relay_recv, att_send, att_recv,
):
    row = lax.axis_index("rows")
    col = lax.axis_index("cols")
    chips = n_cols // cores
    chip, core = col // cores, col % cores
    sibling = chip * cores + (cores - 1 - core)
    band_rows, strip_cols, channels = hidden.shape
    strip = band_rows * strip_cols
    pair = cores * strip
    head_size = w_query.shape[0]
    piece = strip // PIECES
    scale = math.log2(math.e) / math.sqrt(head_size)

    loads = [
        pltpu.make_async_copy(source, target, load_sem.at[index])
        for index, (source, target) in enumerate(
            [
                (hidden_hbm, hidden),
                (gain_hbm, gain),
                (bias_hbm, bias),
                (w_query_hbm, w_query),
                (w_keyval_hbm, w_keyval),
                (w_out_hbm, w_out),
                (out_bias_hbm, out_bias),
            ]
        )
    ]
    for load in loads:
        load.start()

    barrier = pltpu.get_barrier_semaphore()

    def greet_col(step):
        pl.semaphore_signal(
            barrier, inc=1, device_id={"cols": lax.rem(col + step + 1, n_cols)}, device_id_type=MESH
        )

    def greet_row(step):
        pl.semaphore_signal(
            barrier, inc=1, device_id={"rows": lax.rem(row + step + 1, n_rows)}, device_id_type=MESH
        )

    repeat(n_cols - 1, greet_col)
    repeat(n_rows - 1, greet_row)

    def rows_of(core_index, part):
        return pl.ds(pl.multiple_of(core_index * strip + part * piece, piece), piece)

    def strip_copy(step, part):
        other = lax.rem(chip + step + 1, chips)
        block = normed.at[chip, rows_of(core, part), :]
        return pltpu.make_async_remote_copy(
            src_ref=block, dst_ref=block,
            send_sem=strip_send.at[step, part], recv_sem=strip_recv.at[step, part],
            device_id={"cols": other * cores + core}, device_id_type=MESH,
        )

    def relay_copy(step, part):
        source_chip = lax.rem(chip + chips - step, chips)
        block = normed.at[source_chip, rows_of(core, part), :]
        return pltpu.make_async_remote_copy(
            src_ref=block, dst_ref=block,
            send_sem=relay_send.at[step, part], recv_sem=relay_recv.at[step, part],
            device_id={"cols": sibling}, device_id_type=MESH,
        )

    def by_distance(step):
        tables = [sorted(range(n_rows), key=lambda band: (abs(band - at), band))[step] for at in range(n_rows)]
        band = tables[0]
        for at in range(1, n_rows):
            band = jnp.where(row == at, tables[at], band)
        return band

    def band_copy(target):
        return pltpu.make_async_remote_copy(
            src_ref=stale_hbm, dst_ref=keyval.at[row],
            send_sem=band_send.at[target], recv_sem=band_recv.at[row],
            device_id={"rows": target}, device_id_type=MESH,
        )

    def band_arrived(band):
        pltpu.make_async_copy(keyval.at[band], keyval.at[band], band_recv.at[band]).wait()

    pl.semaphore_wait(barrier, n_cols - 1 + n_rows - 1)
    for step in range(1, n_rows):
        band_copy(by_distance(n_rows - step)).start()

    for load in loads[:3]:
        load.wait()
    gains, biases = gain[...].reshape(1, channels), bias[...].reshape(1, channels)
    piece_rows = band_rows // PIECES
    for part in range(PIECES):
        values = hidden[part * piece_rows : (part + 1) * piece_rows].astype(jnp.float32)
        values = values.reshape(piece, channels)
        centred = values - jnp.mean(values, axis=-1, keepdims=True)
        variance = jnp.mean(centred * centred, axis=-1, keepdims=True)
        normed[chip, rows_of(core, part), :] = (
            centred * lax.rsqrt(variance + 1e-05) * gains + biases
        ).astype(jnp.bfloat16)
        repeat(chips - 1, lambda step: strip_copy(step, part).start())
        if cores > 1:
            relay_copy(0, part).start()

    def project(index, part, parts):
        depth = strip // parts
        places = [core_index * strip + part * depth for core_index in range(cores)]
        rows = jnp.concatenate([normed[index, place : place + depth] for place in places], axis=0)
        own = lax.dot_general(
            rows, w_query[...], (((1,), (1,)), ((), ())), preferred_element_type=jnp.float32
        ).astype(jnp.bfloat16)
        own = jnp.concatenate([own, jnp.zeros_like(own)], axis=1)
        both = jnp.dot(rows, w_keyval[...], preferred_element_type=jnp.float32).astype(jnp.bfloat16)
        deep = band_rows // parts
        wide = both.astype(jnp.float32).reshape(cores, deep, strip_cols, both.shape[1])
        for which, place in enumerate(places):
            block = slice(which * depth, (which + 1) * depth)
            queries[index, place : place + depth] = own[block]
            keyval[row, pl.ds(pl.multiple_of(index * pair + place, depth), depth), :] = both[block]
            fresh_wide[part * deep : (part + 1) * deep, index * cores + which] = wide[which]

    for load in loads[3:5]:
        load.wait()
    if cores > 1:
        for part in range(PIECES):
            relay_copy(0, part).wait_recv()
    project(chip, 0, 1)

    def arrive(step):
        def finish(half):
            if cores > 1:
                for part in range(half * PIECES // 2, (half + 1) * PIECES // 2):
                    relay_copy(step + 1, part).wait_recv()
            project(lax.rem(chip + chips - step - 1, chips), half, 2)

        for part in range(PIECES):
            strip_copy(step, part).wait_recv()
            if cores > 1:
                relay_copy(step + 1, part).start()
            if part == PIECES - 2:
                finish(0)
        finish(1)

    repeat(chips - 1, arrive)

    fresh[...] = fresh_wide[...].reshape(fresh.shape).astype(jnp.bfloat16)

    cells = keyval.shape[1]
    together = max(size for size in range(1, n_rows + 1) if n_rows % size == 0 and (size == 1 or size * cells <= 1024))

    def absorb(state, own, band):
        block = keyval[pl.ds(band * together, together)].reshape(together * cells, keyval.shape[2])
        scores = lax.dot_general(
            block, own, (((1,), (1,)), ((), ())), preferred_element_type=jnp.float32
        )
        block_values = block.T[head_size:]
        new_max = jnp.max(scores, axis=0, keepdims=True)
        if state is not None:
            new_max = jnp.maximum(state[0], new_max)
        weights = jnp.exp2((scores - new_max) * scale)
        denominator = jnp.sum(weights, axis=0, keepdims=True)
        weighted = jnp.dot(block_values, weights.astype(jnp.bfloat16), preferred_element_type=jnp.float32)
        if state is not None:
            factor = jnp.exp2((state[0] - new_max) * scale)
            denominator = state[1] * factor + denominator
            weighted = state[2] * factor + weighted
        return new_max, denominator, weighted

    def keep(state, first, count):
        found = (state[2] / state[1]).T.astype(jnp.bfloat16)
        for which in range(count):
            attention[0, first + which] = found[which * strip : (which + 1) * strip]

    def attend(index):
        own = queries[index]
        state = absorb(None, own, 0)
        if together < n_rows:
            state = lax.fori_loop(
                1, n_rows // together, lambda block, state: absorb(state, own, block), state
            )
        keep(state, index * cores, cores)

    for step in range(1, n_rows):
        band_arrived(by_distance(step))

    def att_copy(target, step):
        return pltpu.make_async_remote_copy(
            src_ref=attention.at[0, target], dst_ref=attention.at[1, col],
            send_sem=att_send.at[step], recv_sem=att_recv.at[step],
            device_id={"cols": target}, device_id_type=MESH,
        )

    def serve(step):
        other = lax.rem(chip + step + 1, chips)
        attend(other)
        for which in range(cores):
            target = other * cores + lax.rem(core + which, cores)
            att_copy(target, (step + 1) * cores + which).start()

    repeat(chips - 1, serve)
    attend(chip)
    if cores > 1:
        att_copy(sibling, 1).start()
    attention[1, col] = attention[0, col]

    for load in loads[5:]:
        load.wait()
    if cores > 1:
        att_copy(sibling, 1).wait_recv()

    def heads_of(index):
        heads = jnp.concatenate([attention[1, index * cores + which] for which in range(cores)], axis=1)
        depth = cores * head_size
        weights = w_out[pl.ds(pl.multiple_of(index * depth, depth), depth), :]
        return jnp.dot(heads, weights, preferred_element_type=jnp.float32)

    result = hidden[...].astype(jnp.float32).reshape(strip, channels) + out_bias[...].reshape(1, channels)
    result = result + heads_of(chip)
    for step in range(cores, n_cols):
        att_copy(sibling, step).wait_recv()
    for step in range(1, chips):
        result = result + heads_of(lax.rem(chip + step, chips))
    out[...] = result.reshape(out.shape).astype(jnp.bfloat16)

    for part in range(PIECES):
        repeat(chips - 1, lambda step, part=part: strip_copy(step, part).wait_send())
        if cores > 1:
            repeat(chips, lambda step, part=part: relay_copy(step, part).wait_send())
    for step in range(1, n_rows):
        band_copy(by_distance(step)).wait_send()
    for step in range(1, n_cols):
        att_copy(sibling, step).wait_send()


def write_back(out, fresh, out_hbm, fresh_hbm, store_sem):
    stores = [
        pltpu.make_async_copy(out, out_hbm, store_sem.at[0]),
        pltpu.make_async_copy(fresh, fresh_hbm, store_sem.at[1]),
    ]
    for store in stores:
        store.start()
    for store in stores:
        store.wait()


def shards(n_rows, n_cols, hidden, ln_gain, ln_bias, w_query, w_keyval, stale_keyval, w_out, out_bias):
    band_rows, strip_cols, channels = hidden.shape
    head_size = w_query.shape[1]
    full_cols = stale_keyval.shape[1]
    cells = band_rows * full_cols
    strip = band_rows * strip_cols
    cores = 2 if n_cols % 2 == 0 else 1
    chips = n_cols // cores
    bf16, f32 = jnp.bfloat16, jnp.float32
    near = pl.BlockSpec(memory_space=pltpu.VMEM)
    far = pl.BlockSpec(memory_space=pltpu.HBM)
    dma = pltpu.SemaphoreType.DMA
    operands = (
        hidden,
        ln_gain,
        ln_bias,
        w_query.T,
        w_keyval,
        stale_keyval.reshape(cells, 2 * head_size),
        w_out,
        out_bias,
    )
    shapes = (hidden.shape, (band_rows, full_cols, 2 * head_size))
    found = pl.pallas_call(
        functools.partial(kernel, n_rows, n_cols, cores),
        out_shape=tuple(pltpu.VMEM(shape, bf16) for shape in shapes),
        in_specs=[far] * 8,
        out_specs=(near, near),
        scratch_shapes=[
            pltpu.VMEM(hidden.shape, bf16),
            pltpu.VMEM((channels,), f32),
            pltpu.VMEM((channels,), f32),
            pltpu.VMEM((channels,), f32),
            pltpu.VMEM((head_size, channels), bf16),
            pltpu.VMEM(w_keyval.shape, bf16),
            pltpu.VMEM(w_out.shape, bf16),
            pltpu.VMEM((chips, cores * strip, channels), bf16),
            pltpu.VMEM((chips, cores * strip, 2 * head_size), bf16),
            pltpu.VMEM((n_rows, cells, 2 * head_size), bf16),
            pltpu.VMEM((band_rows, n_cols, strip_cols, 2 * head_size), f32),
            pltpu.VMEM((2, n_cols, strip, head_size), bf16),
            dma((7,)),
            dma((n_rows,)),
            dma((n_rows,)),
            dma((chips, PIECES)),
            dma((chips, PIECES)),
            dma((chips, PIECES)),
            dma((chips, PIECES)),
            dma((n_cols,)),
            dma((n_cols,)),
        ],
        compiler_params=pltpu.CompilerParams(
            collective_id=0, has_side_effects=True, vmem_limit_bytes=48 * 1024 * 1024
        ),
    )(*(pltpu.with_memory_space_constraint(operand, pltpu.HBM) for operand in operands))
    out, fresh = pl.pallas_call(
        write_back,
        out_shape=tuple(pltpu.HBM(shape, bf16) for shape in shapes),
        in_specs=[pl.BlockSpec(memory_space=pl.ANY)] * 2,
        out_specs=(far, far),
        scratch_shapes=[dma((2,))],
        compiler_params=pltpu.CompilerParams(vmem_limit_bytes=2 * 1024 * 1024),
    )(*found)
    return out, fresh.reshape(band_rows, full_cols, 1, 2 * head_size)


def solution(mesh):
    return jax.shard_map(
        functools.partial(shards, mesh.shape["rows"], mesh.shape["cols"]),
        mesh=mesh,
        in_specs=(
            P(("groups", "rows"), "cols", None),
            P(),
            P(),
            P(None, "cols"),
            P(None, "cols"),
            P(("groups", "rows"), None, "cols", None),
            P(),
            P(),
        ),
        out_specs=(P(("groups", "rows"), "cols", None), P(("groups", "rows"), None, "cols", None)),
        check_vma=False,
    )
```
